128 devices in a mesh: seq: 8 (over z, core), expert: 16 (over y, x).
Axes of the slice: x: 4, y: 4, z: 4, core: 2. Of those that a mesh axis runs over, the one named last changes fastest.
Arguments:
- residual: bfloat16 [16, 1024, 2048], P('expert', 'seq'), may hold values from -6 to 6
- queries: bfloat16 [16, 1024, 2048], P('expert', 'seq'), may hold values from -400 to 400
- key_input: bfloat16 [16, 1024, 512], P('expert', 'seq'), may hold values from -4 to 4
- value_input: bfloat16 [16, 1024, 512], P('expert', 'seq'), may hold values from -6 to 6
- routes: int32 [16, 1024, 6], P('expert', 'seq'), may hold values from 0 to 31, all different within a row; in each aligned block of 128 rows (0 to 127, 128 to 255, ..., all dimensions but the last counted through in order) at most 30 rows name the same one
- mix_weights: float32 [16, 1024, 6], P('expert', 'seq'), may hold values from 0.1 to 1
- gate_weight: bfloat16 [32, 2048, 704], P('expert'), may hold values from -0.125 to 0.125
- up_weight: bfloat16 [32, 2048, 704], P('expert'), may hold values from -0.125 to 0.125
- down_weight: bfloat16 [32, 704, 2048], P('expert'), may hold values from -0.21875 to 0.21875
- grad_out: bfloat16 [16, 1024, 2048], P('expert', 'seq'), may hold values from -6 to 6
Outputs:
- layer_out: bfloat16 [16, 1024, 2048], P('expert', 'seq')
- residual_grad: bfloat16 [16, 1024, 2048], P('expert', 'seq')
- query_grad: bfloat16 [16, 1024, 2048], P('expert', 'seq')
- key_grad: bfloat16 [16, 1024, 512], P('expert', 'seq')
- value_grad: bfloat16 [16, 1024, 512], P('expert', 'seq')
- mix_grad: float32 [16, 1024, 6], P('expert', 'seq')
- gate_weight_grad: bfloat16 [32, 2048, 704], P('expert', 'seq')
- up_weight_grad: bfloat16 [32, 2048, 704], P('expert', 'seq')
- down_weight_grad: bfloat16 [32, 704, 2048], P('expert', None, 'seq')
The draws below stay inside these ranges and needn't reach their ends.
Inputs may be any that keep to these rules, and one draw needn't show every extreme that they name: `routes`: each row names 6 different experts. Among the rows of one device no expert is named by more than 30 rows, and in every draw some expert is named by exactly 30 rows of some device.
All inputs are finite; a program needn't handle non-finite values.
Results may differ from the reference program's by a relative error of at most 0.04.
Values may be sent and summed in bfloat16 or wider, within the bound.
No kernel may reach another device: no remote copies, remote signals or barrier semaphores. Data moves between devices by JAX's collectives and lax.ppermute only.
A program may use at most 192 MiB of HBM per device.

```python
import math
import jax
import jax.numpy as jnp
import numpy as np
from jax import lax

D = 2048
HQ = 16
HK = 4
DH = 128
F = 704
TOPK = 6
TOK_DEV = 128
EXPERTS = 32
SEQS = 16
SEQ_LEN = 1024
CAP = 30
N_SEQ = 8


def paired_draws(key):
    key_base = jax.random.fold_in(key, 101)
    query_base = jax.random.fold_in(key, 202)
    key_vectors = jnp.clip(jax.random.normal(key_base, (SEQS, SEQ_LEN, HK, DH), jnp.float32), -4.0, 4.0)
    query_vectors = jnp.clip(jax.random.normal(query_base, (SEQS, SEQ_LEN, HQ, DH), jnp.float32), -4.0, 4.0)
    query_out = query_vectors.reshape(SEQS, SEQ_LEN, HQ * DH).astype(jnp.bfloat16)
    key_out = key_vectors.reshape(SEQS, SEQ_LEN, HK * DH).astype(jnp.bfloat16)
    return (query_out, key_out)


def draw_queries(key, part):
    return paired_draws(key)[0]


def draw_key_input(key, part):
    return paired_draws(key)[1]


def shard_levels(stream_key, shape, pieces, low, largest):
    gain = 1.0
    for axis_at, blocks in pieces:
        steps = jax.random.uniform(jax.random.fold_in(jax.random.fold_in(stream_key, 6), axis_at), (blocks,), jnp.float32, low / len(pieces), largest / len(pieces))
        gain = gain * jnp.repeat(jnp.exp(steps), shape[axis_at] // blocks).reshape((-1,) + (1,) * (len(shape) - 1 - axis_at))
    return gain


def routed_block(own_key, own, number, rows, count, top, bound, lean):
    ranking = jax.random.permutation(own_key, count)
    heavy_load, ordinary = portions_of(count, rows * top, bound, lean, True), portions_of(count, rows * top, bound, lean, False)
    places = jnp.arange(count)

    def named(sizes, turn):
        used = int((sizes > 0).sum())
        fixed = max(1, used // 4)
        moved = fixed + (places - fixed + turn * (used - fixed)) % max(1, count - fixed)
        return jnp.zeros((count,), jnp.int32).at[ranking[jnp.where(places < fixed, places, moved)]].set(jnp.asarray(sizes, jnp.int32))

    sizes = jnp.where(number % 4 == 0, named(heavy_load, number // 4), named(ordinary, number - number // 4 - 1))
    mixed = jax.random.permutation(jax.random.fold_in(own, 3), count)
    giver, sink = mixed[0:count // 2 * 2:2], mixed[1:count // 2 * 2:2]
    margin = jnp.minimum(sizes[giver] - 1, bound - sizes[sink]) // 2
    margin = jnp.where((giver == ranking[0]) | (sink == ranking[0]) | (sizes[sink] == 0), 0, jnp.maximum(margin, 0))
    moved = jax.random.randint(jax.random.fold_in(own, 4), (count // 2,), 0, 1 << 20) % (margin + 1)
    sizes = sizes.at[giver].add(-moved).at[sink].add(moved)
    members = jnp.searchsorted(jnp.cumsum(sizes), jnp.arange(rows * top), side="right").astype(jnp.int32)
    grid = members.reshape(top, rows).T
    grid = grid[jax.random.permutation(jax.random.fold_in(own, 1), rows)]
    turn = jax.random.randint(jax.random.fold_in(own, 2), (rows, 1), 0, top)
    return jnp.take_along_axis(grid, (jnp.arange(top)[None, :] + turn) % top, axis=1)


def portions_of(amount, total, most, slope, full):
    portions = [(1 << 20) // math.isqrt(standing ** slope) + 1 for standing in range(1, amount + 1)]
    largest = most if full else min(most, max(-(-total // amount), total * portions[0] // sum(portions)))
    least = 1 if total - largest >= amount - 1 else 0
    given, surplus = [largest] + [least] * (amount - 1), total - largest - least * (amount - 1)
    while surplus > 0:
        candidates = [i for i in range(1, amount) if given[i] < largest] or [i for i in range(1, amount) if given[i] < most]
        whole, left = sum([portions[i] for i in candidates]), surplus
        for i in candidates:
            more = min(most - given[i], max(1, left * portions[i] // whole), surplus)
            given[i] = given[i] + more
            surplus = surplus - more
    return np.array(given)


def centred(stream_key, dims, deviation, bound, split=(), held_as=jnp.bfloat16):
    values = deviation * jax.random.normal(stream_key, dims, jnp.float32)
    if split:
        values = values * shard_levels(stream_key, dims, split, -0.22, 0.18)
    return jnp.clip(values, -bound, bound).astype(held_as)


def setup_inputs(seed: int = 0) -> dict:
    splits = jax.random.split(jax.random.key(seed), 11)
    residual = centred(splits[0], (SEQS, SEQ_LEN, D), 1.0, 6.0, ((0, 16), (1, 8)))
    queries = draw_queries(jax.random.fold_in(splits[10], 71), 0)
    key_input = draw_key_input(jax.random.fold_in(splits[10], 71), 0)
    value_input = centred(splits[3], (SEQS, SEQ_LEN, HK * DH), 1.0, 6.0, ((0, 16), (1, 8)))
    routes_keys = jax.random.split(jax.random.fold_in(splits[4], 1), SEQS * SEQ_LEN // TOK_DEV)
    routes_turns = jax.random.permutation(jax.random.fold_in(splits[4], 3), SEQS * SEQ_LEN // TOK_DEV)
    routes = jax.vmap(lambda own, number: routed_block(jax.random.fold_in(splits[4], 2), own, number, TOK_DEV, EXPERTS, TOPK, CAP, 2))(routes_keys, routes_turns).reshape((SEQS, SEQ_LEN, TOPK))
    mix_weights = jnp.clip(jnp.exp(math.log(1.0) - 2.3025851 * jax.random.uniform(splits[5], (SEQS, SEQ_LEN, TOPK), jnp.float32) ** shard_levels(splits[5], (SEQS, SEQ_LEN, TOPK), ((0, 16), (1, 8)), -0.2, 0.2)), 0.1, 1.0)
    gate_weight = centred(splits[6], (EXPERTS, D, F), D ** -0.5, 0.125, ((0, 16),))
    up_weight = centred(splits[7], (EXPERTS, D, F), D ** -0.5, 0.125, ((0, 16),))
    down_weight = centred(splits[8], (EXPERTS, F, D), F ** -0.5, 0.21875, ((0, 16),))
    grad_out = centred(splits[9], (SEQS, SEQ_LEN, D), 1.0, 6.0, ((0, 16), (1, 8)))
    return dict(residual=residual, queries=queries, key_input=key_input, value_input=value_input, routes=routes, mix_weights=mix_weights, gate_weight=gate_weight, up_weight=up_weight, down_weight=down_weight, grad_out=grad_out)


neg_big = -1e+30
norm_eps = 1e-06
highest = lax.Precision.HIGHEST

def round_trip(values):
    return lax.optimization_barrier(values.astype(jnp.bfloat16)).astype(jnp.float32)

def causal_scores(query_seq, key_seq):
    length = query_seq.shape[0]
    group_size = HQ // HK
    query_heads = query_seq.astype(jnp.float32).reshape(length, HK, group_size, DH)
    key_heads = key_seq.astype(jnp.float32).reshape(length, HK, DH)
    scores = jnp.einsum('tkgd,jkd->tkgj', query_heads, key_heads, precision=highest) * (1.0 / math.sqrt(DH))
    positions = jnp.arange(length, dtype=jnp.int32)
    visible = (positions[None, :] <= positions[:, None])[:, None, None, :]
    return (query_heads, key_heads, scores, visible)

def attend_forward(operands):
    query_seq, key_seq, value_seq = operands
    length = query_seq.shape[0]
    query_heads, key_heads, scores, visible = causal_scores(query_seq, key_seq)
    value_heads = value_seq.astype(jnp.float32).reshape(length, HK, DH)
    masked = jnp.where(visible, scores, neg_big)
    row_max = lax.optimization_barrier(jnp.max(masked, axis=3))
    weights = jnp.where(visible, jnp.exp(masked - row_max[..., None]), 0.0)
    row_sum = lax.optimization_barrier(jnp.sum(weights, axis=3))
    mixed = jnp.einsum('tkgj,jkd->tkgd', round_trip(weights), value_heads, precision=highest)
    attention = (mixed / row_sum[..., None]).reshape(length, HQ * DH).astype(jnp.bfloat16)
    return (attention, row_max + jnp.log(row_sum))

def attend_backward(operands):
    query_seq, key_seq, value_seq, attention_seq, total_seq, out_grad_seq = operands
    length = query_seq.shape[0]
    group_size = HQ // HK
    inv_scale = 1.0 / math.sqrt(DH)
    query_heads, key_heads, scores, visible = causal_scores(query_seq, key_seq)
    value_heads = value_seq.astype(jnp.float32).reshape(length, HK, DH)
    probabilities = jnp.where(visible, jnp.exp(scores - total_seq[..., None]), 0.0)
    out_grad = out_grad_seq.astype(jnp.float32).reshape(length, HK, group_size, DH)
    attention_heads = attention_seq.astype(jnp.float32).reshape(length, HK, group_size, DH)
    row_delta = lax.optimization_barrier(jnp.sum(out_grad * attention_heads, axis=3))
    prob_grad = jnp.einsum('tkgd,jkd->tkgj', out_grad, value_heads, precision=highest)
    score_grad = round_trip(probabilities * (prob_grad - row_delta[..., None]))
    query_grad = jnp.einsum('tkgj,jkd->tkgd', score_grad, key_heads, precision=highest) * inv_scale
    blocks_shape = (N_SEQ, TOK_DEV, HK, group_size)
    key_part = jnp.einsum('stkgj,stkgd->sjkd', score_grad.reshape(blocks_shape + (length,)), query_heads.reshape(blocks_shape + (DH,)), precision=highest) * inv_scale
    value_part = jnp.einsum('stkgj,stkgd->sjkd', round_trip(probabilities).reshape(blocks_shape + (length,)), out_grad.reshape(blocks_shape + (DH,)), precision=highest)
    key_grad = lax.optimization_barrier(jnp.sum(round_trip(key_part), axis=0)).reshape(length, HK * DH).astype(jnp.bfloat16)
    value_grad = lax.optimization_barrier(jnp.sum(round_trip(value_part), axis=0)).reshape(length, HK * DH).astype(jnp.bfloat16)
    return (query_grad.reshape(length, HQ * DH).astype(jnp.bfloat16), key_grad, value_grad)

def reference(residual, queries, key_input, value_input, routes, mix_weights, gate_weight, up_weight, down_weight, grad_out):
    attention, log_total = lax.map(attend_forward, (queries, key_input, value_input))
    tokens_all = SEQS * SEQ_LEN
    hidden_flat = (residual.astype(jnp.float32) + attention.astype(jnp.float32)).reshape(tokens_all, D)
    inv_rms = lax.rsqrt(lax.optimization_barrier(jnp.mean(hidden_flat * hidden_flat, axis=1, keepdims=True)) + norm_eps)
    normed = hidden_flat * inv_rms
    normed_bf = normed.astype(jnp.bfloat16)
    blocks = tokens_all // TOK_DEV
    route_blocks = routes.reshape(blocks, TOK_DEV, TOPK)
    onehot = (route_blocks[..., None] == jnp.arange(EXPERTS, dtype=jnp.int32)).astype(jnp.int32)
    per_token = lax.optimization_barrier(jnp.sum(onehot, axis=2))
    earlier = jnp.cumsum(per_token, axis=1) - per_token
    slot_rank = lax.optimization_barrier(jnp.sum(onehot * earlier[:, :, None, :], axis=3))
    position = jnp.arange(blocks, dtype=jnp.int32)[:, None, None] * CAP + slot_rank
    pair_ids = jnp.arange(tokens_all * TOPK, dtype=jnp.int32)
    table = jnp.zeros((EXPERTS, blocks * CAP), jnp.int32).at[route_blocks.reshape(-1), position.reshape(-1)].set(pair_ids)
    alive_table = jnp.zeros((EXPERTS, blocks * CAP), jnp.bool_).at[route_blocks.reshape(-1), position.reshape(-1)].set(True)
    mix_flat = mix_weights.reshape(-1)
    grad_flat = grad_out.reshape(tokens_all, D)

    def forward_step(carried, operands):
        combined, mix_grad = carried
        gate_matrix, up_matrix, down_matrix, pairs, alive = operands
        token_ids = pairs // TOPK
        rows = jnp.where(alive[:, None], normed_bf[token_ids], jnp.zeros((), jnp.bfloat16))
        gate_pre = jnp.dot(rows, gate_matrix, preferred_element_type=jnp.float32)
        up_pre = jnp.dot(rows, up_matrix, preferred_element_type=jnp.float32)
        activation = (jax.nn.silu(gate_pre) * up_pre).astype(jnp.bfloat16)
        output = jnp.dot(activation, down_matrix, preferred_element_type=jnp.float32).astype(jnp.bfloat16)
        weight = jnp.where(alive, mix_flat[pairs], 0.0)
        combined = combined.at[token_ids].add(weight[:, None] * output.astype(jnp.float32))
        inner = lax.optimization_barrier(jnp.sum(grad_flat[token_ids].astype(jnp.float32) * output.astype(jnp.float32), axis=1))
        mix_grad = mix_grad.at[pairs].add(jnp.where(alive, inner, 0.0))
        return ((combined, mix_grad), None)
    (combined, mix_grad), ignored = lax.scan(forward_step, (hidden_flat, jnp.zeros((tokens_all * TOPK,), jnp.float32)), (gate_weight, up_weight, down_weight, table, alive_table))

    def backward_step(normed_grad, operands):
        gate_matrix, up_matrix, down_matrix, pairs, alive = operands
        token_ids = pairs // TOPK
        rows = jnp.where(alive[:, None], normed_bf[token_ids], jnp.zeros((), jnp.bfloat16))
        gate_pre = jnp.dot(rows, gate_matrix, preferred_element_type=jnp.float32)
        up_pre = jnp.dot(rows, up_matrix, preferred_element_type=jnp.float32)
        activation = (jax.nn.silu(gate_pre) * up_pre).astype(jnp.bfloat16)
        weight = jnp.where(alive, mix_flat[pairs], 0.0)
        grad_rows = (weight[:, None] * grad_flat[token_ids].astype(jnp.float32)).astype(jnp.bfloat16)
        act_grad = jnp.dot(grad_rows, down_matrix.T, preferred_element_type=jnp.float32)
        sigmoid = jax.nn.sigmoid(gate_pre)
        gate_grad = (act_grad * up_pre * sigmoid * (1.0 + gate_pre * (1.0 - sigmoid))).astype(jnp.bfloat16)
        up_grad = (act_grad * gate_pre * sigmoid).astype(jnp.bfloat16)
        input_grad = (jnp.dot(gate_grad, gate_matrix.T, preferred_element_type=jnp.float32) + jnp.dot(up_grad, up_matrix.T, preferred_element_type=jnp.float32)).astype(jnp.bfloat16)
        normed_grad = normed_grad.at[token_ids].add(jnp.where(alive[:, None], input_grad.astype(jnp.float32), 0.0))
        rows_split = rows.astype(jnp.float32).reshape(SEQS, N_SEQ, CAP, D)
        gate_split = gate_grad.astype(jnp.float32).reshape(SEQS, N_SEQ, CAP, F)
        up_split = up_grad.astype(jnp.float32).reshape(SEQS, N_SEQ, CAP, F)
        act_split = activation.astype(jnp.float32).reshape(SEQS, N_SEQ, CAP, F)
        grad_split = grad_rows.astype(jnp.float32).reshape(SEQS, N_SEQ, CAP, D)
        gate_part = jnp.einsum('jscd,jscf->sdf', rows_split, gate_split, precision=highest)
        up_part = jnp.einsum('jscd,jscf->sdf', rows_split, up_split, precision=highest)
        down_part = jnp.einsum('jscf,jscd->sfd', act_split, grad_split, precision=highest)
        sums = (lax.optimization_barrier(jnp.sum(round_trip(gate_part), axis=0)).astype(jnp.bfloat16), lax.optimization_barrier(jnp.sum(round_trip(up_part), axis=0)).astype(jnp.bfloat16), lax.optimization_barrier(jnp.sum(round_trip(down_part), axis=0)).astype(jnp.bfloat16))
        return (normed_grad, sums)
    normed_grad, weight_sums = lax.scan(backward_step, jnp.zeros((tokens_all, D), jnp.float32), (gate_weight, up_weight, down_weight, table, alive_table))
    dot_mean = lax.optimization_barrier(jnp.mean(normed_grad * normed, axis=1, keepdims=True))
    hidden_grad = grad_flat.astype(jnp.float32) + inv_rms * (normed_grad - normed * dot_mean)
    residual_grad = hidden_grad.astype(jnp.bfloat16).reshape(SEQS, SEQ_LEN, D)
    query_grad, key_grad, value_grad = lax.map(attend_backward, (queries, key_input, value_input, attention, log_total, residual_grad))
    layer_out = combined.astype(jnp.bfloat16).reshape(SEQS, SEQ_LEN, D)
    return (layer_out, residual_grad, query_grad, key_grad, value_grad, mix_grad.reshape(SEQS, SEQ_LEN, TOPK), weight_sums[0], weight_sums[1], weight_sums[2])
```

```python
import math

import jax
import jax.numpy as jnp
from jax import lax
from jax.experimental import pallas as pl
from jax.experimental.pallas import tpu as pltpu
from jax.sharding import PartitionSpec as P

DH = 128
TOK = 128
WIDTH = 2048
HEADS = 16
KV_HEADS = 4
GROUP = 4
KV_WIDTH = 512
TOP = 6
SEQ = 8
PLANES = 4
RANKS = 16
EXPERTS = 32
SLOTS = 32
ROWS = EXPERTS * SLOTS
HIDDEN = 704
FULL = TOK * SEQ
SCALE = 1.0 / math.sqrt(DH)
NEG_BIG = -1e30
NORM_EPS = 1e-06
VMEM_BYTES = 56 * 1024 * 1024

bf16 = jnp.bfloat16
f32 = jnp.float32

PLANE_GROUPS = [
    [(2 * z + core) * RANKS + rank for core in range(2) for rank in range(RANKS)]
    for z in range(PLANES)
]
Z_GROUPS = [[2 * z + core for z in range(PLANES)] for core in range(2)]


def params(**kw):
    return pltpu.CompilerParams(vmem_limit_bytes=VMEM_BYTES, **kw)


def whole(shape):
    return pl.BlockSpec(shape, lambda *_: (0,) * len(shape))


def dot_nn(a, b):
    return lax.dot_general(a, b, (((1,), (0,)), ((), ())), preferred_element_type=f32)


def dot_nt(a, b):
    return lax.dot_general(a, b, (((1,), (1,)), ((), ())), preferred_element_type=f32)


def dot_tn(a, b):
    return lax.dot_general(a, b, (((0,), (0,)), ((), ())), preferred_element_type=f32)


def expert_ids():
    row = lax.broadcasted_iota(jnp.int32, (EXPERTS, TOK), 0)
    return 2 * (row & (RANKS - 1)) + (row >> 4)


def plan_kernel(routes, mix, grad, pick_out, mixed_out, rows_out):
    ids = expert_ids()
    member = jnp.zeros((EXPERTS, TOK), f32)
    weight = jnp.zeros((EXPERTS, TOK), f32)
    for c in range(TOP):
        hit = routes[c : c + 1, :] == ids
        member = member + jnp.where(hit, 1.0, 0.0)
        weight = weight + jnp.where(hit, mix[c : c + 1, :], 0.0)
    before = lax.broadcasted_iota(jnp.int32, (TOK, TOK), 0) < lax.broadcasted_iota(
        jnp.int32, (TOK, TOK), 1
    )
    rank = dot_nn(member.astype(bf16), jnp.where(before, 1.0, 0.0).astype(bf16))
    slot = jnp.where(member > 0.0, rank, -1.0)
    place = lax.broadcasted_iota(jnp.int32, (EXPERTS, SLOTS, TOK), 1).astype(f32)
    pick = jnp.where(slot[:, None, :] == place, 1.0, 0.0)
    mixed = (pick * weight[:, None, :]).reshape(ROWS, TOK)
    pick = pick.reshape(ROWS, TOK)
    pick_out[...] = pick.astype(bf16)
    mixed_out[...] = mixed
    step = 256
    for i in range(0, ROWS, step):
        rows = dot_nn(pick[i : i + step].astype(bf16), grad[...])
        scale = jnp.sum(mixed[i : i + step], axis=1, keepdims=True)
        rows_out[i : i + step, :] = (rows * scale).astype(bf16)


def make_plan(routes, mix, grad):
    return pl.pallas_call(
        plan_kernel,
        out_shape=(
            jax.ShapeDtypeStruct((ROWS, TOK), bf16),
            jax.ShapeDtypeStruct((ROWS, TOK), f32),
            jax.ShapeDtypeStruct((ROWS, WIDTH), bf16),
        ),
        compiler_params=params(),
        cost_estimate=pl.CostEstimate(
            flops=2 * ROWS * TOK * WIDTH, bytes_accessed=8 << 20, transcendentals=0
        ),
    )(routes, mix, grad)


def visible_keys(seq_ref):
    row = seq_ref[0] * TOK + lax.broadcasted_iota(jnp.int32, (TOK, FULL), 0)
    return lax.broadcasted_iota(jnp.int32, (TOK, FULL), 1) <= row


def norm_parts(residual, attention):
    hidden = residual.astype(f32) + attention.astype(f32)
    inv_rms = lax.rsqrt(jnp.mean(hidden * hidden, axis=1, keepdims=True) + NORM_EPS)
    return hidden, inv_rms


def attend_kernel(seq_ref, q_ref, k_ref, v_ref, residual, pick, att_out, lse_out, rows_out):
    head = pl.program_id(0)
    keys, values = k_ref[...], v_ref[...]
    visible = visible_keys(seq_ref)
    outs, totals = [], []
    for g in range(GROUP):
        scores = dot_nt(q_ref[:, g * DH : (g + 1) * DH], keys) * SCALE
        masked = jnp.where(visible, scores, NEG_BIG)
        row_max = jnp.max(masked, axis=1, keepdims=True)
        weights = jnp.exp(masked - row_max)
        row_sum = jnp.sum(weights, axis=1, keepdims=True)
        mixed = dot_nn(weights.astype(bf16), values)
        outs.append((mixed / row_sum).astype(bf16))
        totals.append(jnp.broadcast_to(row_max + jnp.log(row_sum), (TOK, DH)))
    columns = pl.ds(pl.multiple_of(head * GROUP * DH, GROUP * DH), GROUP * DH)
    att_out[:, columns] = jnp.concatenate(outs, axis=1)
    lse_out[...] = jnp.concatenate(totals, axis=1)

    @pl.when(head == KV_HEADS - 1)
    def _():
        hidden, inv_rms = norm_parts(residual[...], att_out[...])
        normed = (hidden * inv_rms).astype(bf16)
        for i in range(0, ROWS, 256):
            rows_out[i : i + 256, :] = dot_nn(pick[i : i + 256, :], normed).astype(bf16)


def attend(seq_index, queries, pairs, residual, pick):
    return pl.pallas_call(
        attend_kernel,
        grid_spec=pltpu.PrefetchScalarGridSpec(
            num_scalar_prefetch=1,
            grid=(KV_HEADS,),
            in_specs=[
                pl.BlockSpec((TOK, GROUP * DH), lambda h, s: (0, h)),
                pl.BlockSpec((FULL, DH), lambda h, s: (0, h)),
                pl.BlockSpec((FULL, DH), lambda h, s: (0, KV_HEADS + h)),
                whole((TOK, WIDTH)),
                whole((ROWS, TOK)),
            ],
            out_specs=[
                whole((TOK, WIDTH)),
                pl.BlockSpec((TOK, GROUP * DH), lambda h, s: (0, h)),
                whole((ROWS, WIDTH)),
            ],
        ),
        out_shape=(
            jax.ShapeDtypeStruct((TOK, WIDTH), bf16),
            jax.ShapeDtypeStruct((TOK, WIDTH), f32),
            jax.ShapeDtypeStruct((ROWS, WIDTH), bf16),
        ),
        compiler_params=params(),
        cost_estimate=pl.CostEstimate(
            flops=4 * TOK * FULL * WIDTH + 2 * ROWS * TOK * WIDTH,
            bytes_accessed=10 << 20,
            transcendentals=HEADS * TOK * FULL,
        ),
    )(seq_index, queries, pairs, pairs, residual, pick)


def expert_kernel(core, rows, pairs, gate_w, up_w, down_w, back_out, act_out, gate_out, up_out):
    gate = dot_nt(rows[...], gate_w[0])
    up = dot_nt(rows[...], up_w[0])
    sig = jax.nn.sigmoid(gate)
    silu = gate * sig
    act_out[...] = (silu * up).astype(bf16)
    act_grad = dot_nt(pairs[...], down_w[0])
    gate_grad = (act_grad * up * sig * (1.0 + gate * (1.0 - sig))).astype(bf16)
    up_grad = (act_grad * silu).astype(bf16)
    gate_out[...] = gate_grad
    up_out[...] = up_grad
    back_out[...] = (dot_nn(gate_grad, gate_w[0]) + dot_nn(up_grad, up_w[0])).astype(bf16)


def expert_rows(core, rows, pairs, gate_w, up_w, down_w):
    step = 256
    tile = pl.BlockSpec((step, WIDTH), lambda i, c: (i, 0))
    thin = pl.BlockSpec((step, HIDDEN), lambda i, c: (i, 0))
    weight = pl.BlockSpec((1, HIDDEN, WIDTH), lambda i, c: (c[0], 0, 0))
    return pl.pallas_call(
        expert_kernel,
        grid_spec=pltpu.PrefetchScalarGridSpec(
            num_scalar_prefetch=1,
            grid=(ROWS // step,),
            in_specs=[tile, tile, weight, weight, weight],
            out_specs=[tile, thin, thin, thin],
        ),
        out_shape=(
            jax.ShapeDtypeStruct((ROWS, WIDTH), bf16),
            jax.ShapeDtypeStruct((ROWS, HIDDEN), bf16),
            jax.ShapeDtypeStruct((ROWS, HIDDEN), bf16),
            jax.ShapeDtypeStruct((ROWS, HIDDEN), bf16),
        ),
        compiler_params=params(),
        cost_estimate=pl.CostEstimate(
            flops=10 * ROWS * HIDDEN * WIDTH,
            bytes_accessed=24 << 20,
            transcendentals=ROWS * HIDDEN,
        ),
    )(core, rows, pairs, gate_w, up_w, down_w)


def sums_kernel(rows, pairs, act, gate, up, gate_out, up_out, down_out):
    gate_out[0] = dot_tn(gate[...], rows[...]).astype(bf16)
    up_out[0] = dot_tn(up[...], rows[...]).astype(bf16)
    down_out[0] = dot_tn(act[...], pairs[...]).astype(bf16)


def weight_sums(rows, pairs, act, gate, up):
    part = WIDTH // PLANES
    columns = pl.BlockSpec((ROWS, part), lambda i: (0, i))
    thin = whole((ROWS, HIDDEN))
    out = pl.BlockSpec((1, HIDDEN, part), lambda i: (i, 0, 0))
    shape = jax.ShapeDtypeStruct((PLANES, HIDDEN, part), bf16)
    return pl.pallas_call(
        sums_kernel,
        grid=(PLANES,),
        in_specs=[columns, columns, thin, thin, thin],
        out_specs=[out, out, out],
        out_shape=(shape, shape, shape),
        compiler_params=params(),
        cost_estimate=pl.CostEstimate(
            flops=6 * ROWS * HIDDEN * WIDTH, bytes_accessed=22 << 20, transcendentals=0
        ),
    )(rows, pairs, act, gate, up)


def result_kernel(core, act, down_w, out):
    out[...] = dot_nn(act[...], down_w[0]).astype(bf16)


def expert_results(core, act, down_w):
    step = 256
    return pl.pallas_call(
        result_kernel,
        grid_spec=pltpu.PrefetchScalarGridSpec(
            num_scalar_prefetch=1,
            grid=(ROWS // step,),
            in_specs=[
                pl.BlockSpec((step, HIDDEN), lambda i, c: (i, 0)),
                pl.BlockSpec((1, HIDDEN, WIDTH), lambda i, c: (c[0], 0, 0)),
            ],
            out_specs=pl.BlockSpec((step, WIDTH), lambda i, c: (i, 0)),
        ),
        out_shape=jax.ShapeDtypeStruct((ROWS, WIDTH), bf16),
        compiler_params=params(),
        cost_estimate=pl.CostEstimate(
            flops=2 * ROWS * HIDDEN * WIDTH, bytes_accessed=9 << 20, transcendentals=0
        ),
    )(core, act, down_w)


def attend_back_kernel(
    seq_ref, q_ref, k_ref, v_ref, lse, back, pick, residual, att, grad, res_out, q_out, kv_out
):
    head = pl.program_id(0)

    @pl.when(head == 0)
    def _():
        normed_grad = dot_tn(pick[...], back[...])
        hidden, inv_rms = norm_parts(residual[...], att[...])
        normed = hidden * inv_rms
        dot_mean = jnp.mean(normed_grad * normed, axis=1, keepdims=True)
        total = grad[...].astype(f32) + inv_rms * (normed_grad - normed * dot_mean)
        res_out[...] = total.astype(bf16)

    keys, values = k_ref[...], v_ref[...]
    visible = visible_keys(seq_ref)
    score_parts, prob_parts, query_parts, grad_parts = [], [], [], []
    for g in range(GROUP):
        query = q_ref[:, g * DH : (g + 1) * DH]
        columns = pl.ds(pl.multiple_of(head * GROUP * DH + g * DH, DH), DH)
        out_grad = res_out[:, columns]
        delta = jnp.sum(
            out_grad.astype(f32) * att[:, columns].astype(f32), axis=1, keepdims=True
        )
        scores = dot_nt(query, keys) * SCALE
        total = lse[:, g * DH : g * DH + 1]
        probs = jnp.exp(jnp.where(visible, scores - total, NEG_BIG))
        prob_grad = dot_nt(out_grad, values)
        score_grad = (probs * (prob_grad - delta)).astype(bf16)
        q_out[:, g * DH : (g + 1) * DH] = (dot_nn(score_grad, keys) * SCALE).astype(bf16)
        score_parts.append(score_grad)
        prob_parts.append(probs.astype(bf16))
        query_parts.append(query)
        grad_parts.append(out_grad)
    key_sum = dot_tn(jnp.concatenate(score_parts, axis=0), jnp.concatenate(query_parts, axis=0))
    value_sum = dot_tn(jnp.concatenate(prob_parts, axis=0), jnp.concatenate(grad_parts, axis=0))
    kv_out[:, pl.ds(pl.multiple_of(head * DH, DH), DH)] = (key_sum * SCALE).astype(bf16)
    kv_out[:, pl.ds(pl.multiple_of(KV_WIDTH + head * DH, DH), DH)] = value_sum.astype(bf16)


def attend_back(seq_index, queries, pairs, lse, back, pick, residual, att, grad):
    return pl.pallas_call(
        attend_back_kernel,
        grid_spec=pltpu.PrefetchScalarGridSpec(
            num_scalar_prefetch=1,
            grid=(KV_HEADS,),
            in_specs=[
                pl.BlockSpec((TOK, GROUP * DH), lambda h, s: (0, h)),
                pl.BlockSpec((FULL, DH), lambda h, s: (0, h)),
                pl.BlockSpec((FULL, DH), lambda h, s: (0, KV_HEADS + h)),
                pl.BlockSpec((TOK, GROUP * DH), lambda h, s: (0, h)),
                whole((ROWS, WIDTH)),
                whole((ROWS, TOK)),
                whole((TOK, WIDTH)),
                whole((TOK, WIDTH)),
                whole((TOK, WIDTH)),
            ],
            out_specs=[
                whole((TOK, WIDTH)),
                pl.BlockSpec((TOK, GROUP * DH), lambda h, s: (0, h)),
                whole((FULL, 2 * KV_WIDTH)),
            ],
        ),
        out_shape=(
            jax.ShapeDtypeStruct((TOK, WIDTH), bf16),
            jax.ShapeDtypeStruct((TOK, WIDTH), bf16),
            jax.ShapeDtypeStruct((FULL, 2 * KV_WIDTH), bf16),
        ),
        compiler_params=params(),
        cost_estimate=pl.CostEstimate(
            flops=10 * TOK * FULL * WIDTH + 2 * ROWS * TOK * WIDTH,
            bytes_accessed=12 << 20,
            transcendentals=HEADS * TOK * FULL,
        ),
    )(seq_index, queries, pairs, pairs, lse, back, pick, residual, att, grad)


def combine_kernel(routes, pick, mixed, returned, residual, att, grad, layer_out, mix_out):
    hidden = residual[...].astype(f32) + att[...].astype(f32)
    coarse = mixed[...].astype(bf16)
    fine = (mixed[...] - coarse.astype(f32)).astype(bf16)
    total = hidden + dot_tn(coarse, returned[...]) + dot_tn(fine, returned[...])
    layer_out[...] = total.astype(bf16)
    sums = []
    for i in range(0, ROWS, 256):
        rows = dot_nn(pick[i : i + 256, :], grad[...])
        inner = jnp.sum(rows * returned[i : i + 256, :].astype(f32), axis=1, keepdims=True)
        spread = pick[i : i + 256, :].astype(f32) * inner
        sums.append(jnp.sum(spread.reshape(256 // SLOTS, SLOTS, TOK), axis=1))
    by_expert = jnp.concatenate(sums, axis=0)
    ids = expert_ids()
    for c in range(TOP):
        hit = routes[c : c + 1, :] == ids
        mix_out[c : c + 1, :] = jnp.sum(jnp.where(hit, by_expert, 0.0), axis=0, keepdims=True)


def combine(routes, pick, mixed, returned, residual, att, grad):
    return pl.pallas_call(
        combine_kernel,
        out_shape=(
            jax.ShapeDtypeStruct((TOK, WIDTH), bf16),
            jax.ShapeDtypeStruct((TOP, TOK), f32),
        ),
        compiler_params=params(),
        cost_estimate=pl.CostEstimate(
            flops=6 * ROWS * TOK * WIDTH, bytes_accessed=8 << 20, transcendentals=0
        ),
    )(routes, pick, mixed, returned, residual, att, grad)


def exchange(rows):
    blocks = rows.reshape(EXPERTS, SLOTS, WIDTH)
    moved = lax.all_to_all(
        blocks, ("seq", "expert"), 0, 0, tiled=True, axis_index_groups=PLANE_GROUPS
    )
    return moved.reshape(ROWS, WIDTH)


def swap_cores(values):
    return lax.ppermute(values, "seq", [(i, i ^ 1) for i in range(SEQ)])


def on_device(
    residual,
    queries,
    key_input,
    value_input,
    routes,
    mix_weights,
    gate_weight,
    up_weight,
    down_weight,
    grad_out,
):
    seq = lax.axis_index("seq")
    seq_index = seq.astype(jnp.int32).reshape(1)
    core = (seq & 1).astype(jnp.int32)
    core_index = core.reshape(1)
    residual = residual.reshape(TOK, WIDTH)
    queries = queries.reshape(TOK, WIDTH)
    grad = grad_out.reshape(TOK, WIDTH)
    routes = routes.reshape(TOK, TOP).T
    mix = mix_weights.reshape(TOK, TOP).T
    gate_w = jnp.swapaxes(gate_weight, 1, 2)
    up_w = jnp.swapaxes(up_weight, 1, 2)
    pairs = jnp.concatenate(
        [key_input.reshape(TOK, KV_WIDTH), value_input.reshape(TOK, KV_WIDTH)], axis=1
    )
    pairs = lax.all_gather(pairs, "seq", axis=0, tiled=True)
    pick, mixed, grad_rows = make_plan(routes, mix, grad)
    grad_rows = exchange(grad_rows)
    att, lse, rows = attend(seq_index, queries, pairs, residual, pick)
    rows = exchange(rows)
    back, act, gate_grad, up_grad = expert_rows(
        core_index, rows, grad_rows, gate_w, up_w, down_weight
    )
    back = exchange(back)
    sums = weight_sums(rows, grad_rows, act, gate_grad, up_grad)
    results = expert_results(core_index, act, down_weight)
    res_grad, query_grad, kv_parts = attend_back(
        seq_index, queries, pairs, lse, back, pick, residual, att, grad
    )
    kv_parts = lax.all_to_all(kv_parts.reshape(SEQ, TOK, 2 * KV_WIDTH), "seq", 0, 0, tiled=True)
    kv_grad = jnp.sum(kv_parts.astype(f32), axis=0).astype(bf16)
    results = exchange(results)
    layer_out, mix_grad = combine(routes, pick, mixed, results, residual, att, grad)
    shares = [
        lax.psum_scatter(s, "seq", scatter_dimension=0, axis_index_groups=Z_GROUPS) for s in sums
    ]
    weight_grads = []
    for share in shares:
        low, high = share[:, :256], share[:, 256:]
        mine = jnp.where(core == 0, low, high)
        other = swap_cores(jnp.where(core == 0, high, low))
        weight_grads.append(
            jnp.stack([jnp.where(core == 0, mine, other), jnp.where(core == 0, other, mine)])
        )
    return (
        layer_out.reshape(1, TOK, WIDTH),
        res_grad.reshape(1, TOK, WIDTH),
        query_grad.reshape(1, TOK, WIDTH),
        kv_grad[:, :KV_WIDTH].reshape(1, TOK, KV_WIDTH),
        kv_grad[:, KV_WIDTH:].reshape(1, TOK, KV_WIDTH),
        mix_grad.T.reshape(1, TOK, TOP),
        jnp.swapaxes(weight_grads[0], 1, 2),
        jnp.swapaxes(weight_grads[1], 1, 2),
        weight_grads[2],
    )


def solution(mesh):
    rows = P("expert", "seq", None)
    weights = P("expert", None, None)
    return jax.shard_map(
        on_device,
        mesh=mesh,
        in_specs=(rows, rows, rows, rows, rows, rows, weights, weights, weights, rows),
        out_specs=(rows, rows, rows, rows, rows, rows, rows, rows, P("expert", None, "seq")),
        check_vma=False,
    )
```

```python
import math

import jax
import jax.numpy as jnp
from jax import lax
from jax.experimental import pallas as pl
from jax.experimental.pallas import tpu as pltpu
from jax.sharding import PartitionSpec as P

DH = 128
TOK = 128
WIDTH = 2048
HEADS = 16
KV_HEADS = 4
GROUP = 4
KV_WIDTH = 512
TOP = 6
SEQ = 8
PLANES = 4
RANKS = 16
EXPERTS = 32
SLOTS = 32
HALF = 16
ROWS = EXPERTS * SLOTS
PART = EXPERTS * HALF
OWN = WIDTH // SEQ
HIDDEN = 704
FULL = TOK * SEQ
SCALE = 1.0 / math.sqrt(DH)
NEG_BIG = -1e30
NORM_EPS = 1e-06
VMEM_BYTES = 56 * 1024 * 1024

bf16 = jnp.bfloat16
f32 = jnp.float32

PLANE_GROUPS = [
    [(2 * z + core) * RANKS + rank for core in range(2) for rank in range(RANKS)]
    for z in range(PLANES)
]
Z_GROUPS = [[2 * z + core for z in range(PLANES)] for core in range(2)]


def params(**kw):
    return pltpu.CompilerParams(vmem_limit_bytes=VMEM_BYTES, **kw)


def cost(share, flops, bytes_accessed, transcendentals):
    return pl.CostEstimate(
        flops=share * flops, bytes_accessed=share * bytes_accessed, transcendentals=transcendentals
    )


def whole(shape):
    return pl.BlockSpec(shape, lambda *_: (0,) * len(shape))


def dot_nn(a, b):
    return lax.dot_general(a, b, (((1,), (0,)), ((), ())), preferred_element_type=f32)


def dot_nt(a, b):
    return lax.dot_general(a, b, (((1,), (1,)), ((), ())), preferred_element_type=f32)


def dot_tn(a, b):
    return lax.dot_general(a, b, (((0,), (0,)), ((), ())), preferred_element_type=f32)


def expert_ids():
    row = lax.broadcasted_iota(jnp.int32, (EXPERTS, TOK), 0)
    return 2 * (row & (RANKS - 1)) + (row >> 4)


def plan_kernel(routes, mix, grad, pick_out, mixed_out, rows_out):
    ids = expert_ids()
    member = jnp.zeros((EXPERTS, TOK), f32)
    weight = jnp.zeros((EXPERTS, TOK), f32)
    for c in range(TOP):
        hit = routes[c] == ids
        member = member + jnp.where(hit, 1.0, 0.0)
        weight = weight + jnp.where(hit, mix[c], 0.0)
    before = lax.broadcasted_iota(jnp.int32, (TOK, TOK), 0) < lax.broadcasted_iota(
        jnp.int32, (TOK, TOK), 1
    )
    rank = dot_nn(member.astype(bf16), jnp.where(before, 1.0, 0.0).astype(bf16))
    slot = jnp.where(member > 0.0, rank, -1.0)
    place = lax.broadcasted_iota(jnp.int32, (EXPERTS, HALF, TOK), 1).astype(f32)
    for h in range(2):
        pick = jnp.where(slot[:, None, :] == place + float(h * HALF), 1.0, 0.0)
        mixed = (pick * weight[:, None, :]).reshape(PART, TOK)
        pick = pick.reshape(PART, TOK).astype(bf16)
        pick_out[h] = pick
        mixed_out[h] = mixed
        scale = jnp.sum(mixed, axis=1, keepdims=True)
        for i in range(0, PART, 256):
            rows = dot_nn(pick[i : i + 256], grad[...])
            rows = (rows * scale[i : i + 256]).astype(bf16)
            first = i // HALF
            rows_out[first : first + 256 // HALF, h] = rows.reshape(256 // HALF, HALF, WIDTH)


def make_plan(routes, mix, grad):
    return pl.pallas_call(
        plan_kernel,
        out_shape=(
            jax.ShapeDtypeStruct((2, PART, TOK), bf16),
            jax.ShapeDtypeStruct((2, PART, TOK), f32),
            jax.ShapeDtypeStruct((EXPERTS, 2, HALF, WIDTH), bf16),
        ),
        compiler_params=params(),
        cost_estimate=cost(5,
            flops=2 * ROWS * TOK * WIDTH, bytes_accessed=8 << 20, transcendentals=0
        ),
    )(routes, mix, grad)


def visible_keys(seq_ref):
    row = seq_ref[0] * TOK + lax.broadcasted_iota(jnp.int32, (TOK, FULL), 0)
    return lax.broadcasted_iota(jnp.int32, (TOK, FULL), 1) <= row


def norm_parts(residual, attention):
    hidden = residual.astype(f32) + attention.astype(f32)
    inv_rms = lax.rsqrt(jnp.mean(hidden * hidden, axis=1, keepdims=True) + NORM_EPS)
    return hidden, inv_rms


def attend_kernel(
    seq_ref, q_ref, k_ref, v_ref, residual, pick, att_out, lse_out, first_out, second_out
):
    head = pl.program_id(0)
    keys, values = k_ref[...], v_ref[...]
    visible = visible_keys(seq_ref)
    outs, totals = [], []
    for g in range(GROUP):
        scores = dot_nt(q_ref[:, g * DH : (g + 1) * DH], keys) * SCALE
        masked = jnp.where(visible, scores, NEG_BIG)
        row_max = jnp.max(masked, axis=1, keepdims=True)
        weights = jnp.exp(masked - row_max)
        row_sum = jnp.sum(weights, axis=1, keepdims=True)
        mixed = dot_nn(weights.astype(bf16), values)
        outs.append((mixed / row_sum).astype(bf16))
        totals.append(jnp.broadcast_to(row_max + jnp.log(row_sum), (TOK, DH)))
    columns = pl.ds(pl.multiple_of(head * GROUP * DH, GROUP * DH), GROUP * DH)
    att_out[:, columns] = jnp.concatenate(outs, axis=1)
    lse_out[...] = jnp.concatenate(totals, axis=1)

    @pl.when(head == KV_HEADS - 1)
    def _():
        hidden, inv_rms = norm_parts(residual[...], att_out[...])
        normed = (hidden * inv_rms).astype(bf16)
        for h, rows_out in enumerate((first_out, second_out)):
            for i in range(0, PART, 256):
                rows_out[i : i + 256, :] = dot_nn(pick[h, i : i + 256, :], normed).astype(bf16)


def attend(seq_index, queries, pairs, residual, pick):
    return pl.pallas_call(
        attend_kernel,
        grid_spec=pltpu.PrefetchScalarGridSpec(
            num_scalar_prefetch=1,
            grid=(KV_HEADS,),
            in_specs=[
                pl.BlockSpec((TOK, GROUP * DH), lambda h, s: (0, h)),
                pl.BlockSpec((FULL, DH), lambda h, s: (0, h)),
                pl.BlockSpec((FULL, DH), lambda h, s: (0, KV_HEADS + h)),
                whole((TOK, WIDTH)),
                whole((2, PART, TOK)),
            ],
            out_specs=[
                whole((TOK, WIDTH)),
                pl.BlockSpec((TOK, GROUP * DH), lambda h, s: (0, h)),
                whole((PART, WIDTH)),
                whole((PART, WIDTH)),
            ],
        ),
        out_shape=(
            jax.ShapeDtypeStruct((TOK, WIDTH), bf16),
            jax.ShapeDtypeStruct((TOK, WIDTH), f32),
            jax.ShapeDtypeStruct((PART, WIDTH), bf16),
            jax.ShapeDtypeStruct((PART, WIDTH), bf16),
        ),
        compiler_params=params(),
        cost_estimate=cost(5,
            flops=4 * TOK * FULL * WIDTH + 2 * ROWS * TOK * WIDTH,
            bytes_accessed=10 << 20,
            transcendentals=HEADS * TOK * FULL,
        ),
    )(seq_index, queries, pairs, pairs, residual, pick)


def expert_kernel(core, rows, pairs, gate_w, up_w, down_w, back_out, act_out, gate_out, up_out):
    step = rows.shape[0]
    gate = dot_nt(rows[...], gate_w[0])
    up = dot_nt(rows[...], up_w[0])
    sig = jax.nn.sigmoid(gate)
    silu = gate * sig
    act_out[...] = (silu * up).astype(bf16)
    act_grad = dot_nt(pairs[...].reshape(step, WIDTH), down_w[0])
    gate_grad = (act_grad * up * sig * (1.0 + gate * (1.0 - sig))).astype(bf16)
    up_grad = (act_grad * silu).astype(bf16)
    gate_out[...] = gate_grad
    up_out[...] = up_grad
    back_out[...] = (dot_nn(gate_grad, gate_w[0]) + dot_nn(up_grad, up_w[0])).astype(bf16)


def expert_rows(half, core, rows, pairs, gate_w, up_w, down_w):
    step = 256
    tile = pl.BlockSpec((step, WIDTH), lambda i, c: (i, 0))
    thin = pl.BlockSpec((step, HIDDEN), lambda i, c: (i, 0))
    weight = pl.BlockSpec(
        (1, HIDDEN, WIDTH), lambda i, c: (c[0], 0, 0), pipeline_mode=pl.Buffered(1)
    )
    return pl.pallas_call(
        expert_kernel,
        grid_spec=pltpu.PrefetchScalarGridSpec(
            num_scalar_prefetch=1,
            grid=(PART // step,),
            in_specs=[
                tile,
                pl.BlockSpec((step // HALF, 1, HALF, WIDTH), lambda i, c: (i, half, 0, 0)),
                weight,
                weight,
                weight,
            ],
            out_specs=[tile, thin, thin, thin],
        ),
        out_shape=(
            jax.ShapeDtypeStruct((PART, WIDTH), bf16),
            jax.ShapeDtypeStruct((PART, HIDDEN), bf16),
            jax.ShapeDtypeStruct((PART, HIDDEN), bf16),
            jax.ShapeDtypeStruct((PART, HIDDEN), bf16),
        ),
        compiler_params=params(),
        cost_estimate=cost(100,
            flops=10 * PART * HIDDEN * WIDTH,
            bytes_accessed=16 << 20,
            transcendentals=PART * HIDDEN,
        ),
    )(core, rows, pairs, gate_w, up_w, down_w)


def split_columns(place, total, value, keep_out, send_out):
    total[...] = value
    keep = pl.ds(pl.multiple_of(place * OWN, OWN), OWN)
    send = pl.ds(pl.multiple_of((1 - place) * OWN, OWN), OWN)
    keep_out[0] = total[:, keep].astype(bf16)
    send_out[0] = total[:, send].astype(bf16)


def down_kernel(core, pairs, act_a, act_b, keep, send, total):
    pairs_a = pairs[:, 0].reshape(PART, 2 * OWN)
    pairs_b = pairs[:, 1].reshape(PART, 2 * OWN)
    value = dot_tn(act_a[...], pairs_a) + dot_tn(act_b[...], pairs_b)
    split_columns(core[0], total, value, keep, send)


def inner_kernel(
    core, rows_a, rows_b, gate_a, gate_b, up_a, up_b, gate_keep, gate_send, up_keep, up_send, total
):
    value = dot_tn(gate_a[...], rows_a[...]) + dot_tn(gate_b[...], rows_b[...])
    split_columns(core[0], total, value, gate_keep, gate_send)
    value = dot_tn(up_a[...], rows_a[...]) + dot_tn(up_b[...], rows_b[...])
    split_columns(core[0], total, value, up_keep, up_send)


def column_sums(kernel, n_outs, core, wide, thin):
    columns = [
        pl.BlockSpec((PART, 2 * OWN), lambda i, c: (0, i))
        if w.ndim == 2
        else pl.BlockSpec((EXPERTS, 2, HALF, 2 * OWN), lambda i, c: (0, 0, 0, i))
        for w in wide
    ]
    out = pl.BlockSpec((1, HIDDEN, OWN), lambda i, c: (i, 0, 0))
    return pl.pallas_call(
        kernel,
        grid_spec=pltpu.PrefetchScalarGridSpec(
            num_scalar_prefetch=1,
            grid=(PLANES,),
            in_specs=columns + [whole((PART, HIDDEN))] * len(thin),
            out_specs=[out] * n_outs,
            scratch_shapes=[pltpu.VMEM((HIDDEN, 2 * OWN), f32)],
        ),
        out_shape=(jax.ShapeDtypeStruct((PLANES, HIDDEN, OWN), bf16),) * n_outs,
        compiler_params=params(),
        cost_estimate=cost(100,
            flops=n_outs * ROWS * HIDDEN * WIDTH,
            bytes_accessed=n_outs * (4 << 20),
            transcendentals=0,
        ),
    )(core, *wide, *thin)


def stack_kernel(core, keep, other, out):
    out[0, core[0]] = keep[0]
    out[0, 1 - core[0]] = other[0]


def stack_experts(core, keep, other):
    block = pl.BlockSpec((1, HIDDEN, OWN), lambda i, c: (i, 0, 0))
    return pl.pallas_call(
        stack_kernel,
        grid_spec=pltpu.PrefetchScalarGridSpec(
            num_scalar_prefetch=1,
            grid=(PLANES,),
            in_specs=[block, block],
            out_specs=pl.BlockSpec((1, 2, HIDDEN, OWN), lambda i, c: (i, 0, 0, 0)),
        ),
        out_shape=jax.ShapeDtypeStruct((PLANES, 2, HIDDEN, OWN), bf16),
        compiler_params=params(),
        cost_estimate=cost(100, flops=0, bytes_accessed=6 << 20, transcendentals=0),
    )(core, keep, other)


def result_kernel(core, act_a, act_b, down_w, out):
    rows = act_a.shape[0]
    out[:, 0] = dot_nn(act_a[...], down_w[0]).astype(bf16).reshape(rows // HALF, HALF, WIDTH)
    out[:, 1] = dot_nn(act_b[...], down_w[0]).astype(bf16).reshape(rows // HALF, HALF, WIDTH)


def expert_results(core, act, down_w):
    step = 128
    return pl.pallas_call(
        result_kernel,
        grid_spec=pltpu.PrefetchScalarGridSpec(
            num_scalar_prefetch=1,
            grid=(PART // step,),
            in_specs=[
                pl.BlockSpec((step, HIDDEN), lambda i, c: (i, 0)),
                pl.BlockSpec((step, HIDDEN), lambda i, c: (i, 0)),
                pl.BlockSpec((1, HIDDEN, WIDTH), lambda i, c: (c[0], 0, 0)),
            ],
            out_specs=pl.BlockSpec((step // HALF, 2, HALF, WIDTH), lambda i, c: (i, 0, 0, 0)),
        ),
        out_shape=jax.ShapeDtypeStruct((EXPERTS, 2, HALF, WIDTH), bf16),
        compiler_params=params(),
        cost_estimate=cost(100,
            flops=2 * ROWS * HIDDEN * WIDTH, bytes_accessed=9 << 20, transcendentals=0
        ),
    )(core, *act, down_w)


def attend_back_kernel(
    seq_ref,
    q_ref,
    k_ref,
    v_ref,
    lse,
    back_a,
    back_b,
    pick,
    residual,
    att,
    grad,
    res_out,
    q_out,
    keep_out,
    send_out,
    kv_sum,
):
    head = pl.program_id(0)

    @pl.when(head == 0)
    def _():
        normed_grad = dot_tn(pick[0], back_a[...]) + dot_tn(pick[1], back_b[...])
        hidden, inv_rms = norm_parts(residual[...], att[...])
        normed = hidden * inv_rms
        dot_mean = jnp.mean(normed_grad * normed, axis=1, keepdims=True)
        total = grad[...].astype(f32) + inv_rms * (normed_grad - normed * dot_mean)
        res_out[...] = total.astype(bf16)

    keys, values = k_ref[...], v_ref[...]
    visible = visible_keys(seq_ref)
    score_parts, prob_parts, query_parts, grad_parts = [], [], [], []
    for g in range(GROUP):
        query = q_ref[:, g * DH : (g + 1) * DH]
        columns = pl.ds(pl.multiple_of(head * GROUP * DH + g * DH, DH), DH)
        out_grad = res_out[:, columns]
        delta = jnp.sum(
            out_grad.astype(f32) * att[:, columns].astype(f32), axis=1, keepdims=True
        )
        scores = dot_nt(query, keys) * SCALE
        total = lse[:, g * DH : g * DH + 1]
        probs = jnp.exp(jnp.where(visible, scores - total, NEG_BIG))
        prob_grad = dot_nt(out_grad, values)
        score_grad = (probs * (prob_grad - delta)).astype(bf16)
        q_out[:, g * DH : (g + 1) * DH] = (dot_nn(score_grad, keys) * SCALE).astype(bf16)
        score_parts.append(score_grad)
        prob_parts.append(probs.astype(bf16))
        query_parts.append(query)
        grad_parts.append(out_grad)
    key_sum = dot_tn(jnp.concatenate(score_parts, axis=0), jnp.concatenate(query_parts, axis=0))
    value_sum = dot_tn(jnp.concatenate(prob_parts, axis=0), jnp.concatenate(grad_parts, axis=0))
    kv_sum[:, pl.ds(pl.multiple_of(head * DH, DH), DH)] = (key_sum * SCALE).astype(bf16)
    kv_sum[:, pl.ds(pl.multiple_of(KV_WIDTH + head * DH, DH), DH)] = value_sum.astype(bf16)

    @pl.when(head == KV_HEADS - 1)
    def _():
        plane, core = seq_ref[0] >> 1, seq_ref[0] & 1
        for d in range(PLANES):
            mine = 2 * ((plane + d) & (PLANES - 1)) + core
            keep_out[d] = kv_sum[pl.ds(pl.multiple_of(mine * TOK, TOK), TOK), :]
            send_out[d] = kv_sum[pl.ds(pl.multiple_of((mine ^ 1) * TOK, TOK), TOK), :]


def attend_back(seq_index, queries, pairs, lse, back_a, back_b, pick, residual, att, grad):
    return pl.pallas_call(
        attend_back_kernel,
        grid_spec=pltpu.PrefetchScalarGridSpec(
            num_scalar_prefetch=1,
            grid=(KV_HEADS,),
            in_specs=[
                pl.BlockSpec((TOK, GROUP * DH), lambda h, s: (0, h)),
                pl.BlockSpec((FULL, DH), lambda h, s: (0, h)),
                pl.BlockSpec((FULL, DH), lambda h, s: (0, KV_HEADS + h)),
                pl.BlockSpec((TOK, GROUP * DH), lambda h, s: (0, h)),
                whole((PART, WIDTH)),
                whole((PART, WIDTH)),
                whole((2, PART, TOK)),
                whole((TOK, WIDTH)),
                whole((TOK, WIDTH)),
                whole((TOK, WIDTH)),
            ],
            out_specs=[
                whole((TOK, WIDTH)),
                pl.BlockSpec((TOK, GROUP * DH), lambda h, s: (0, h)),
                whole((PLANES, TOK, 2 * KV_WIDTH)),
                whole((PLANES, TOK, 2 * KV_WIDTH)),
            ],
            scratch_shapes=[pltpu.VMEM((FULL, 2 * KV_WIDTH), bf16)],
        ),
        out_shape=(
            jax.ShapeDtypeStruct((TOK, WIDTH), bf16),
            jax.ShapeDtypeStruct((TOK, WIDTH), bf16),
            jax.ShapeDtypeStruct((PLANES, TOK, 2 * KV_WIDTH), bf16),
            jax.ShapeDtypeStruct((PLANES, TOK, 2 * KV_WIDTH), bf16),
        ),
        compiler_params=params(),
        cost_estimate=cost(100,
            flops=10 * TOK * FULL * WIDTH + 2 * ROWS * TOK * WIDTH,
            bytes_accessed=12 << 20,
            transcendentals=HEADS * TOK * FULL,
        ),
    )(seq_index, queries, pairs, pairs, lse, back_a, back_b, pick, residual, att, grad)


def combine_kernel(routes, pick, mixed, returned, residual, att, grad, layer_out, mix_out):
    total = residual[...].astype(f32) + att[...].astype(f32)
    by_expert = jnp.zeros((EXPERTS, TOK), f32)
    for h in range(2):
        rows = returned[:, h].reshape(PART, WIDTH)
        coarse = mixed[h].astype(bf16)
        fine = (mixed[h] - coarse.astype(f32)).astype(bf16)
        total = total + dot_tn(coarse, rows) + dot_tn(fine, rows)
        inner = dot_nt(rows, grad[...]) * pick[h].astype(f32)
        by_expert = by_expert + jnp.sum(inner.reshape(EXPERTS, HALF, TOK), axis=1)
    layer_out[...] = total.astype(bf16)
    ids = expert_ids()
    for c in range(TOP):
        hit = routes[c] == ids
        mix_out[c] = jnp.sum(jnp.where(hit, by_expert, 0.0), axis=0, keepdims=True)


def combine(routes, pick, mixed, returned, residual, att, grad):
    return pl.pallas_call(
        combine_kernel,
        out_shape=(
            jax.ShapeDtypeStruct((TOK, WIDTH), bf16),
            jax.ShapeDtypeStruct((TOP, 1, TOK), f32),
        ),
        compiler_params=params(),
        cost_estimate=cost(100,
            flops=6 * ROWS * TOK * WIDTH, bytes_accessed=8 << 20, transcendentals=0
        ),
    )(routes, pick, mixed, returned, residual, att, grad)


def pass_kernel(*refs):
    pass


def after(earlier, *values):
    anywhere = pl.BlockSpec(memory_space=pl.ANY)
    return pl.pallas_call(
        pass_kernel,
        in_specs=[anywhere] * (1 + len(values)),
        out_specs=[anywhere] * len(values),
        out_shape=[jax.ShapeDtypeStruct(v.shape, v.dtype) for v in values],
        input_output_aliases={1 + i: i for i in range(len(values))},
    )(earlier, *values)


def exchange(blocks):
    return lax.all_to_all(
        blocks, ("seq", "expert"), 0, 0, tiled=True, axis_index_groups=PLANE_GROUPS
    )


def exchange_rows(rows):
    return exchange(rows.reshape(EXPERTS, HALF, WIDTH)).reshape(PART, WIDTH)


def swap_cores(values):
    return lax.ppermute(values, "seq", [(i, i ^ 1) for i in range(SEQ)])


def send_earlier(values, planes):
    pairs = [
        (2 * z + core, 2 * (z + planes - PLANES) + core)
        for z in range(PLANES - planes, PLANES)
        for core in range(2)
    ]
    return lax.ppermute(values, "seq", pairs)


def on_device(
    residual,
    queries,
    key_input,
    value_input,
    routes,
    mix_weights,
    gate_weight,
    up_weight,
    down_weight,
    grad_out,
):
    seq = lax.axis_index("seq")
    seq_index = seq.astype(jnp.int32).reshape(1)
    core = (seq & 1).astype(jnp.int32)
    core_index = core.reshape(1)
    residual = residual.reshape(TOK, WIDTH)
    queries = queries.reshape(TOK, WIDTH)
    grad = grad_out.reshape(TOK, WIDTH)
    routes = jnp.transpose(routes, (2, 0, 1))
    mix = jnp.transpose(mix_weights, (2, 0, 1))
    gate_w = jnp.swapaxes(gate_weight, 1, 2)
    up_w = jnp.swapaxes(up_weight, 1, 2)
    pairs = jnp.concatenate(
        [key_input.reshape(TOK, KV_WIDTH), value_input.reshape(TOK, KV_WIDTH)], axis=1
    )
    pairs = lax.all_gather(pairs, "seq", axis=0, tiled=True)
    pick, mixed, grad_rows = make_plan(routes, mix, grad)
    grad_rows = exchange(grad_rows)
    att, lse, rows_a, rows_b = attend(seq_index, queries, pairs, residual, pick)
    rows_a, rows_b = after(grad_rows, rows_a, rows_b)
    rows_a, rows_b = exchange_rows(rows_a), exchange_rows(rows_b)
    weights = (gate_w, up_w, down_weight)
    back_a, act_a, gate_a, up_a = expert_rows(0, core_index, rows_a, grad_rows, *weights)
    back_a = exchange_rows(back_a)
    back_b, act_b, gate_b, up_b = expert_rows(1, core_index, rows_b, grad_rows, *weights)
    back_b = exchange_rows(back_b)
    down_keep, down_send = column_sums(down_kernel, 2, core_index, (grad_rows,), (act_a, act_b))
    down_stack = stack_experts(core_index, down_keep, swap_cores(down_send))
    gate_a, gate_b = after(down_stack, gate_a, gate_b)
    gate_keep, gate_send, up_keep, up_send = column_sums(
        inner_kernel, 4, core_index, (rows_a, rows_b), (gate_a, gate_b, up_a, up_b)
    )
    results = exchange(expert_results(core_index, (act_a, act_b), down_weight))
    gate_stack = stack_experts(core_index, gate_keep, swap_cores(gate_send))
    up_stack = stack_experts(core_index, up_keep, swap_cores(up_send))
    (lse,) = after(gate_stack, lse)
    (lse,) = after(up_stack, lse)
    res_grad, query_grad, keep, send = attend_back(
        seq_index, queries, pairs, lse, back_a, back_b, pick, residual, att, grad
    )
    other = swap_cores(send)
    parts = [
        (keep[d].astype(f32) + other[d].astype(f32)).astype(bf16) for d in range(PLANES)
    ]
    kv_grad = parts[0].astype(f32)
    for d in range(1, PLANES):
        kv_grad = kv_grad + send_earlier(parts[d], d).astype(f32)
    kv_grad = kv_grad.astype(bf16)
    layer_out, mix_grad = combine(routes, pick, mixed, results, residual, att, grad)
    weight_grads = []
    for stacked in (down_stack, gate_stack, up_stack):
        share = lax.psum_scatter(
            stacked.reshape(PLANES * 2 * HIDDEN, OWN),
            "seq",
            scatter_dimension=0,
            axis_index_groups=Z_GROUPS,
            tiled=True,
        )
        weight_grads.append(share.reshape(2, HIDDEN, OWN))
    down_grad, gate_grad, up_grad = weight_grads
    return (
        layer_out.reshape(1, TOK, WIDTH),
        res_grad.reshape(1, TOK, WIDTH),
        query_grad.reshape(1, TOK, WIDTH),
        kv_grad[:, :KV_WIDTH].reshape(1, TOK, KV_WIDTH),
        kv_grad[:, KV_WIDTH:].reshape(1, TOK, KV_WIDTH),
        jnp.transpose(mix_grad, (1, 2, 0)),
        jnp.swapaxes(gate_grad, 1, 2),
        jnp.swapaxes(up_grad, 1, 2),
        down_grad,
    )


def solution(mesh):
    rows = P("expert", "seq", None)
    weights = P("expert", None, None)
    return jax.shard_map(
        on_device,
        mesh=mesh,
        in_specs=(rows, rows, rows, rows, rows, rows, weights, weights, weights, rows),
        out_specs=(rows, rows, rows, rows, rows, rows, rows, rows, P("expert", None, "seq")),
        check_vma=False,
    )
```

```python
import math

import jax
import jax.numpy as jnp
from jax import lax
from jax.experimental import pallas as pl
from jax.experimental.pallas import tpu as pltpu
from jax.sharding import PartitionSpec as P

DH = 128
TOK = 128
WIDTH = 2048
HEADS = 16
KV_HEADS = 4
GROUP = 4
KV_WIDTH = 512
TOP = 6
SEQ = 8
PLANES = 4
RANKS = 16
EXPERTS = 32
SLOTS = 32
HALF = 16
ROWS = EXPERTS * SLOTS
PART = EXPERTS * HALF
OWN = WIDTH // SEQ
HIDDEN = 704
FULL = TOK * SEQ
SCALE = 1.0 / math.sqrt(DH)
NEG_BIG = -1e30
NORM_EPS = 1e-06
VMEM_BYTES = 56 * 1024 * 1024

bf16 = jnp.bfloat16
f32 = jnp.float32

PLANE_GROUPS = [
    [(2 * z + core) * RANKS + rank for core in range(2) for rank in range(RANKS)]
    for z in range(PLANES)
]
Z_GROUPS = [[2 * z + core for z in range(PLANES)] for core in range(2)]


def params(**kw):
    return pltpu.CompilerParams(vmem_limit_bytes=VMEM_BYTES, **kw)


def cost(share, flops, bytes_accessed, transcendentals):
    return pl.CostEstimate(
        flops=share * flops, bytes_accessed=share * bytes_accessed, transcendentals=transcendentals
    )


def whole(shape):
    return pl.BlockSpec(shape, lambda *_: (0,) * len(shape))


def dot_nn(a, b):
    return lax.dot_general(a, b, (((1,), (0,)), ((), ())), preferred_element_type=f32)


def dot_nt(a, b):
    return lax.dot_general(a, b, (((1,), (1,)), ((), ())), preferred_element_type=f32)


def dot_tn(a, b):
    return lax.dot_general(a, b, (((0,), (0,)), ((), ())), preferred_element_type=f32)


def expert_ids():
    row = lax.broadcasted_iota(jnp.int32, (EXPERTS, TOK), 0)
    return 2 * (row & (RANKS - 1)) + (row >> 4)


def plan_kernel(routes, mix, grad, pick_out, mixed_out, rows_out):
    ids = expert_ids()
    member = jnp.zeros((EXPERTS, TOK), f32)
    weight = jnp.zeros((EXPERTS, TOK), f32)
    for c in range(TOP):
        hit = routes[c] == ids
        member = member + jnp.where(hit, 1.0, 0.0)
        weight = weight + jnp.where(hit, mix[c], 0.0)
    before = lax.broadcasted_iota(jnp.int32, (TOK, TOK), 0) < lax.broadcasted_iota(
        jnp.int32, (TOK, TOK), 1
    )
    rank = dot_nn(member.astype(bf16), jnp.where(before, 1.0, 0.0).astype(bf16))
    slot = jnp.where(member > 0.0, rank, -1.0)
    place = lax.broadcasted_iota(jnp.int32, (EXPERTS, HALF, TOK), 1).astype(f32)
    for h in range(2):
        pick = jnp.where(slot[:, None, :] == place + float(h * HALF), 1.0, 0.0)
        mixed = (pick * weight[:, None, :]).reshape(PART, TOK)
        pick = pick.reshape(PART, TOK).astype(bf16)
        pick_out[h] = pick
        mixed_out[h] = mixed
        scale = jnp.sum(mixed, axis=1, keepdims=True)
        for i in range(0, PART, 256):
            rows = dot_nn(pick[i : i + 256], grad[...])
            rows = (rows * scale[i : i + 256]).astype(bf16)
            first = i // HALF
            rows_out[first : first + 256 // HALF, h] = rows.reshape(256 // HALF, HALF, WIDTH)


def make_plan(routes, mix, grad):
    return pl.pallas_call(
        plan_kernel,
        out_shape=(
            jax.ShapeDtypeStruct((2, PART, TOK), bf16),
            jax.ShapeDtypeStruct((2, PART, TOK), f32),
            jax.ShapeDtypeStruct((EXPERTS, 2, HALF, WIDTH), bf16),
        ),
        compiler_params=params(),
        cost_estimate=cost(5,
            flops=2 * ROWS * TOK * WIDTH, bytes_accessed=8 << 20, transcendentals=0
        ),
    )(routes, mix, grad)


def visible_keys(seq_ref):
    row = seq_ref[0] * TOK + lax.broadcasted_iota(jnp.int32, (TOK, FULL), 0)
    return lax.broadcasted_iota(jnp.int32, (TOK, FULL), 1) <= row


def norm_parts(residual, attention):
    hidden = residual.astype(f32) + attention.astype(f32)
    inv_rms = lax.rsqrt(jnp.mean(hidden * hidden, axis=1, keepdims=True) + NORM_EPS)
    return hidden, inv_rms


def attend_kernel(
    seq_ref, q_ref, k_ref, v_ref, residual, pick, att_out, lse_out, first_out, second_out
):
    head = pl.program_id(0)
    keys, values = k_ref[...], v_ref[...]
    visible = visible_keys(seq_ref)
    outs, totals = [], []
    for g in range(GROUP):
        scores = dot_nt(q_ref[:, g * DH : (g + 1) * DH], keys) * SCALE
        masked = jnp.where(visible, scores, NEG_BIG)
        row_max = jnp.max(masked, axis=1, keepdims=True)
        weights = jnp.exp(masked - row_max)
        row_sum = jnp.sum(weights, axis=1, keepdims=True)
        mixed = dot_nn(weights.astype(bf16), values)
        outs.append((mixed / row_sum).astype(bf16))
        totals.append(jnp.broadcast_to(row_max + jnp.log(row_sum), (TOK, DH)))
    columns = pl.ds(pl.multiple_of(head * GROUP * DH, GROUP * DH), GROUP * DH)
    att_out[:, columns] = jnp.concatenate(outs, axis=1)
    lse_out[...] = jnp.concatenate(totals, axis=1)

    @pl.when(head == KV_HEADS - 1)
    def _():
        hidden, inv_rms = norm_parts(residual[...], att_out[...])
        normed = (hidden * inv_rms).astype(bf16)
        for h, rows_out in enumerate((first_out, second_out)):
            for i in range(0, PART, 256):
                rows_out[i : i + 256, :] = dot_nn(pick[h, i : i + 256, :], normed).astype(bf16)


def attend(seq_index, queries, pairs, residual, pick):
    return pl.pallas_call(
        attend_kernel,
        grid_spec=pltpu.PrefetchScalarGridSpec(
            num_scalar_prefetch=1,
            grid=(KV_HEADS,),
            in_specs=[
                pl.BlockSpec((TOK, GROUP * DH), lambda h, s: (0, h)),
                pl.BlockSpec((FULL, DH), lambda h, s: (0, h)),
                pl.BlockSpec((FULL, DH), lambda h, s: (0, KV_HEADS + h)),
                whole((TOK, WIDTH)),
                whole((2, PART, TOK)),
            ],
            out_specs=[
                whole((TOK, WIDTH)),
                pl.BlockSpec((TOK, GROUP * DH), lambda h, s: (0, h)),
                whole((PART, WIDTH)),
                whole((PART, WIDTH)),
            ],
        ),
        out_shape=(
            jax.ShapeDtypeStruct((TOK, WIDTH), bf16),
            jax.ShapeDtypeStruct((TOK, WIDTH), f32),
            jax.ShapeDtypeStruct((PART, WIDTH), bf16),
            jax.ShapeDtypeStruct((PART, WIDTH), bf16),
        ),
        compiler_params=params(),
        cost_estimate=cost(5,
            flops=4 * TOK * FULL * WIDTH + 2 * ROWS * TOK * WIDTH,
            bytes_accessed=10 << 20,
            transcendentals=HEADS * TOK * FULL,
        ),
    )(seq_index, queries, pairs, pairs, residual, pick)


def expert_kernel(core, rows, pairs, gate_w, up_w, down_w, back_out, act_out, gate_out, up_out):
    step = rows.shape[0]
    gate = dot_nt(rows[...], gate_w[0])
    up = dot_nt(rows[...], up_w[0])
    sig = jax.nn.sigmoid(gate)
    silu = gate * sig
    act_out[...] = (silu * up).astype(bf16)
    act_grad = dot_nt(pairs[...].reshape(step, WIDTH), down_w[0])
    gate_grad = (act_grad * up * sig * (1.0 + gate * (1.0 - sig))).astype(bf16)
    up_grad = (act_grad * silu).astype(bf16)
    gate_out[...] = gate_grad
    up_out[...] = up_grad
    back_out[...] = (dot_nn(gate_grad, gate_w[0]) + dot_nn(up_grad, up_w[0])).astype(bf16)


def expert_rows(half, core, rows, pairs, gate_w, up_w, down_w):
    step = 256
    tile = pl.BlockSpec((step, WIDTH), lambda i, c: (i, 0))
    thin = pl.BlockSpec((step, HIDDEN), lambda i, c: (i, 0))
    weight = pl.BlockSpec(
        (1, HIDDEN, WIDTH), lambda i, c: (c[0], 0, 0), pipeline_mode=pl.Buffered(1)
    )
    return pl.pallas_call(
        expert_kernel,
        grid_spec=pltpu.PrefetchScalarGridSpec(
            num_scalar_prefetch=1,
            grid=(PART // step,),
            in_specs=[
                tile,
                pl.BlockSpec((step // HALF, 1, HALF, WIDTH), lambda i, c: (i, half, 0, 0)),
                weight,
                weight,
                weight,
            ],
            out_specs=[tile, thin, thin, thin],
        ),
        out_shape=(
            jax.ShapeDtypeStruct((PART, WIDTH), bf16),
            jax.ShapeDtypeStruct((PART, HIDDEN), bf16),
            jax.ShapeDtypeStruct((PART, HIDDEN), bf16),
            jax.ShapeDtypeStruct((PART, HIDDEN), bf16),
        ),
        compiler_params=params(),
        cost_estimate=cost(100,
            flops=10 * PART * HIDDEN * WIDTH,
            bytes_accessed=16 << 20,
            transcendentals=PART * HIDDEN,
        ),
    )(core, rows, pairs, gate_w, up_w, down_w)


def forward_kernel(core, rows, gate_w, up_w, gate_out, up_out, act_out):
    gate = dot_nt(rows[...], gate_w[0])
    up = dot_nt(rows[...], up_w[0])
    gate_out[...] = gate
    up_out[...] = up
    act_out[...] = (gate * jax.nn.sigmoid(gate) * up).astype(bf16)


def backward_kernel(core, gate_in, up_in, pairs, gate_w, up_w, down_w, back_out, gate_out, up_out):
    step = gate_in.shape[0]
    gate, up = gate_in[...], up_in[...]
    sig = jax.nn.sigmoid(gate)
    act_grad = dot_nt(pairs[...].reshape(step, WIDTH), down_w[0])
    gate_grad = (act_grad * up * sig * (1.0 + gate * (1.0 - sig))).astype(bf16)
    up_grad = (act_grad * gate * sig).astype(bf16)
    gate_out[...] = gate_grad
    up_out[...] = up_grad
    back_out[...] = (dot_nn(gate_grad, gate_w[0]) + dot_nn(up_grad, up_w[0])).astype(bf16)


def expert_forward(core, rows, gate_w, up_w):
    step = 256
    thin = pl.BlockSpec((step, HIDDEN), lambda i, c: (i, 0))
    weight = pl.BlockSpec(
        (1, HIDDEN, WIDTH), lambda i, c: (c[0], 0, 0), pipeline_mode=pl.Buffered(1)
    )
    return pl.pallas_call(
        forward_kernel,
        grid_spec=pltpu.PrefetchScalarGridSpec(
            num_scalar_prefetch=1,
            grid=(PART // step,),
            in_specs=[pl.BlockSpec((step, WIDTH), lambda i, c: (i, 0)), weight, weight],
            out_specs=[thin, thin, thin],
        ),
        out_shape=(
            jax.ShapeDtypeStruct((PART, HIDDEN), f32),
            jax.ShapeDtypeStruct((PART, HIDDEN), f32),
            jax.ShapeDtypeStruct((PART, HIDDEN), bf16),
        ),
        compiler_params=params(),
        cost_estimate=cost(100,
            flops=4 * PART * HIDDEN * WIDTH,
            bytes_accessed=10 << 20,
            transcendentals=PART * HIDDEN,
        ),
    )(core, rows, gate_w, up_w)


def expert_backward(half, core, gate, up, pairs, gate_w, up_w, down_w):
    step = 256
    tile = pl.BlockSpec((step, WIDTH), lambda i, c: (i, 0))
    thin = pl.BlockSpec((step, HIDDEN), lambda i, c: (i, 0))
    weight = pl.BlockSpec(
        (1, HIDDEN, WIDTH), lambda i, c: (c[0], 0, 0), pipeline_mode=pl.Buffered(1)
    )
    return pl.pallas_call(
        backward_kernel,
        grid_spec=pltpu.PrefetchScalarGridSpec(
            num_scalar_prefetch=1,
            grid=(PART // step,),
            in_specs=[
                thin,
                thin,
                pl.BlockSpec((step // HALF, 1, HALF, WIDTH), lambda i, c: (i, half, 0, 0)),
                weight,
                weight,
                weight,
            ],
            out_specs=[tile, thin, thin],
        ),
        out_shape=(
            jax.ShapeDtypeStruct((PART, WIDTH), bf16),
            jax.ShapeDtypeStruct((PART, HIDDEN), bf16),
            jax.ShapeDtypeStruct((PART, HIDDEN), bf16),
        ),
        compiler_params=params(),
        cost_estimate=cost(100,
            flops=6 * PART * HIDDEN * WIDTH,
            bytes_accessed=16 << 20,
            transcendentals=PART * HIDDEN,
        ),
    )(core, gate, up, pairs, gate_w, up_w, down_w)


def split_columns(place, total, value, keep_out, send_out):
    total[...] = value
    keep = pl.ds(pl.multiple_of(place * OWN, OWN), OWN)
    send = pl.ds(pl.multiple_of((1 - place) * OWN, OWN), OWN)
    keep_out[0] = total[:, keep].astype(bf16)
    send_out[0] = total[:, send].astype(bf16)


def down_kernel(core, pairs, act_a, act_b, keep, send, total):
    pairs_a = pairs[:, 0].reshape(PART, 2 * OWN)
    pairs_b = pairs[:, 1].reshape(PART, 2 * OWN)
    value = dot_tn(act_a[...], pairs_a) + dot_tn(act_b[...], pairs_b)
    split_columns(core[0], total, value, keep, send)


def inner_kernel(
    core, rows_a, rows_b, gate_a, gate_b, up_a, up_b, gate_keep, gate_send, up_keep, up_send, total
):
    value = dot_tn(gate_a[...], rows_a[...]) + dot_tn(gate_b[...], rows_b[...])
    split_columns(core[0], total, value, gate_keep, gate_send)
    value = dot_tn(up_a[...], rows_a[...]) + dot_tn(up_b[...], rows_b[...])
    split_columns(core[0], total, value, up_keep, up_send)


def column_sums(kernel, n_outs, core, wide, thin):
    columns = [
        pl.BlockSpec((PART, 2 * OWN), lambda i, c: (0, i))
        if w.ndim == 2
        else pl.BlockSpec((EXPERTS, 2, HALF, 2 * OWN), lambda i, c: (0, 0, 0, i))
        for w in wide
    ]
    out = pl.BlockSpec((1, HIDDEN, OWN), lambda i, c: (i, 0, 0))
    return pl.pallas_call(
        kernel,
        grid_spec=pltpu.PrefetchScalarGridSpec(
            num_scalar_prefetch=1,
            grid=(PLANES,),
            in_specs=columns + [whole((PART, HIDDEN))] * len(thin),
            out_specs=[out] * n_outs,
            scratch_shapes=[pltpu.VMEM((HIDDEN, 2 * OWN), f32)],
        ),
        out_shape=(jax.ShapeDtypeStruct((PLANES, HIDDEN, OWN), bf16),) * n_outs,
        compiler_params=params(),
        cost_estimate=cost(100,
            flops=n_outs * ROWS * HIDDEN * WIDTH,
            bytes_accessed=n_outs * (4 << 20),
            transcendentals=0,
        ),
    )(core, *wide, *thin)


def stack_kernel(core, keep, other, out):
    out[0, core[0]] = keep[0]
    out[0, 1 - core[0]] = other[0]


def stack_experts(core, keep, other):
    block = pl.BlockSpec((1, HIDDEN, OWN), lambda i, c: (i, 0, 0))
    return pl.pallas_call(
        stack_kernel,
        grid_spec=pltpu.PrefetchScalarGridSpec(
            num_scalar_prefetch=1,
            grid=(PLANES,),
            in_specs=[block, block],
            out_specs=pl.BlockSpec((1, 2, HIDDEN, OWN), lambda i, c: (i, 0, 0, 0)),
        ),
        out_shape=jax.ShapeDtypeStruct((PLANES, 2, HIDDEN, OWN), bf16),
        compiler_params=params(),
        cost_estimate=cost(100, flops=0, bytes_accessed=6 << 20, transcendentals=0),
    )(core, keep, other)


def result_kernel(core, act_a, act_b, down_w, out):
    rows = act_a.shape[0]
    out[:, 0] = dot_nn(act_a[...], down_w[0]).astype(bf16).reshape(rows // HALF, HALF, WIDTH)
    out[:, 1] = dot_nn(act_b[...], down_w[0]).astype(bf16).reshape(rows // HALF, HALF, WIDTH)


def expert_results(core, act, down_w):
    step = 128
    return pl.pallas_call(
        result_kernel,
        grid_spec=pltpu.PrefetchScalarGridSpec(
            num_scalar_prefetch=1,
            grid=(PART // step,),
            in_specs=[
                pl.BlockSpec((step, HIDDEN), lambda i, c: (i, 0)),
                pl.BlockSpec((step, HIDDEN), lambda i, c: (i, 0)),
                pl.BlockSpec((1, HIDDEN, WIDTH), lambda i, c: (c[0], 0, 0)),
            ],
            out_specs=pl.BlockSpec((step // HALF, 2, HALF, WIDTH), lambda i, c: (i, 0, 0, 0)),
        ),
        out_shape=jax.ShapeDtypeStruct((EXPERTS, 2, HALF, WIDTH), bf16),
        compiler_params=params(),
        cost_estimate=cost(100,
            flops=2 * ROWS * HIDDEN * WIDTH, bytes_accessed=9 << 20, transcendentals=0
        ),
    )(core, *act, down_w)


def attend_back_kernel(
    seq_ref,
    q_ref,
    k_ref,
    v_ref,
    lse,
    back_a,
    back_b,
    pick,
    residual,
    att,
    grad,
    res_out,
    q_out,
    keep_out,
    send_out,
    kv_sum,
):
    head = pl.program_id(0)

    @pl.when(head == 0)
    def _():
        normed_grad = dot_tn(pick[0], back_a[...]) + dot_tn(pick[1], back_b[...])
        hidden, inv_rms = norm_parts(residual[...], att[...])
        normed = hidden * inv_rms
        dot_mean = jnp.mean(normed_grad * normed, axis=1, keepdims=True)
        total = grad[...].astype(f32) + inv_rms * (normed_grad - normed * dot_mean)
        res_out[...] = total.astype(bf16)

    keys, values = k_ref[...], v_ref[...]
    visible = visible_keys(seq_ref)
    score_parts, prob_parts, query_parts, grad_parts = [], [], [], []
    for g in range(GROUP):
        query = q_ref[:, g * DH : (g + 1) * DH]
        columns = pl.ds(pl.multiple_of(head * GROUP * DH + g * DH, DH), DH)
        out_grad = res_out[:, columns]
        delta = jnp.sum(
            out_grad.astype(f32) * att[:, columns].astype(f32), axis=1, keepdims=True
        )
        scores = dot_nt(query, keys) * SCALE
        total = lse[:, g * DH : g * DH + 1]
        probs = jnp.exp(jnp.where(visible, scores - total, NEG_BIG))
        prob_grad = dot_nt(out_grad, values)
        score_grad = (probs * (prob_grad - delta)).astype(bf16)
        q_out[:, g * DH : (g + 1) * DH] = (dot_nn(score_grad, keys) * SCALE).astype(bf16)
        score_parts.append(score_grad)
        prob_parts.append(probs.astype(bf16))
        query_parts.append(query)
        grad_parts.append(out_grad)
    key_sum = dot_tn(jnp.concatenate(score_parts, axis=0), jnp.concatenate(query_parts, axis=0))
    value_sum = dot_tn(jnp.concatenate(prob_parts, axis=0), jnp.concatenate(grad_parts, axis=0))
    kv_sum[:, pl.ds(pl.multiple_of(head * DH, DH), DH)] = (key_sum * SCALE).astype(bf16)
    kv_sum[:, pl.ds(pl.multiple_of(KV_WIDTH + head * DH, DH), DH)] = value_sum.astype(bf16)

    @pl.when(head == KV_HEADS - 1)
    def _():
        plane, core = seq_ref[0] >> 1, seq_ref[0] & 1
        for d in range(PLANES):
            mine = 2 * ((plane + d) & (PLANES - 1)) + core
            keep_out[d] = kv_sum[pl.ds(pl.multiple_of(mine * TOK, TOK), TOK), :]
            send_out[d] = kv_sum[pl.ds(pl.multiple_of((mine ^ 1) * TOK, TOK), TOK), :]


def attend_back(seq_index, queries, pairs, lse, back_a, back_b, pick, residual, att, grad):
    return pl.pallas_call(
        attend_back_kernel,
        grid_spec=pltpu.PrefetchScalarGridSpec(
            num_scalar_prefetch=1,
            grid=(KV_HEADS,),
            in_specs=[
                pl.BlockSpec((TOK, GROUP * DH), lambda h, s: (0, h)),
                pl.BlockSpec((FULL, DH), lambda h, s: (0, h)),
                pl.BlockSpec((FULL, DH), lambda h, s: (0, KV_HEADS + h)),
                pl.BlockSpec((TOK, GROUP * DH), lambda h, s: (0, h)),
                whole((PART, WIDTH)),
                whole((PART, WIDTH)),
                whole((2, PART, TOK)),
                whole((TOK, WIDTH)),
                whole((TOK, WIDTH)),
                whole((TOK, WIDTH)),
            ],
            out_specs=[
                whole((TOK, WIDTH)),
                pl.BlockSpec((TOK, GROUP * DH), lambda h, s: (0, h)),
                whole((PLANES, TOK, 2 * KV_WIDTH)),
                whole((PLANES, TOK, 2 * KV_WIDTH)),
            ],
            scratch_shapes=[pltpu.VMEM((FULL, 2 * KV_WIDTH), bf16)],
        ),
        out_shape=(
            jax.ShapeDtypeStruct((TOK, WIDTH), bf16),
            jax.ShapeDtypeStruct((TOK, WIDTH), bf16),
            jax.ShapeDtypeStruct((PLANES, TOK, 2 * KV_WIDTH), bf16),
            jax.ShapeDtypeStruct((PLANES, TOK, 2 * KV_WIDTH), bf16),
        ),
        compiler_params=params(),
        cost_estimate=cost(100,
            flops=10 * TOK * FULL * WIDTH + 2 * ROWS * TOK * WIDTH,
            bytes_accessed=12 << 20,
            transcendentals=HEADS * TOK * FULL,
        ),
    )(seq_index, queries, pairs, pairs, lse, back_a, back_b, pick, residual, att, grad)


def combine_kernel(
    routes, pick, mixed, returned, residual, att, grad, layer_out, mix_out, by_expert
):
    step = pl.program_id(0)

    @pl.when(step == 0)
    def _():
        by_expert[...] = jnp.zeros_like(by_expert)

    total = residual[...].astype(f32) + att[...].astype(f32)
    for h in range(2):
        rows = returned[:, h].reshape(PART, -1)
        coarse = mixed[h].astype(bf16)
        fine = (mixed[h] - coarse.astype(f32)).astype(bf16)
        total = total + dot_tn(coarse, rows) + dot_tn(fine, rows)
        inner = dot_nt(rows, grad[...]) * pick[h].astype(f32)
        by_expert[...] += jnp.sum(inner.reshape(EXPERTS, HALF, TOK), axis=1)
    layer_out[...] = total.astype(bf16)

    @pl.when(step == pl.num_programs(0) - 1)
    def _():
        ids = expert_ids()
        for c in range(TOP):
            hit = routes[c] == ids
            mix_out[c] = jnp.sum(jnp.where(hit, by_expert[...], 0.0), axis=0, keepdims=True)


def combine(routes, pick, mixed, returned, residual, att, grad):
    part = WIDTH // 4
    columns = pl.BlockSpec((TOK, part), lambda i: (0, i))
    return pl.pallas_call(
        combine_kernel,
        grid=(4,),
        in_specs=[
            whole((TOP, 1, TOK)),
            whole((2, PART, TOK)),
            whole((2, PART, TOK)),
            pl.BlockSpec((EXPERTS, 2, HALF, part), lambda i: (0, 0, 0, i)),
            columns,
            columns,
            columns,
        ],
        out_specs=[columns, whole((TOP, 1, TOK))],
        out_shape=(
            jax.ShapeDtypeStruct((TOK, WIDTH), bf16),
            jax.ShapeDtypeStruct((TOP, 1, TOK), f32),
        ),
        scratch_shapes=[pltpu.VMEM((EXPERTS, TOK), f32)],
        compiler_params=params(),
        cost_estimate=cost(
            100, flops=6 * ROWS * TOK * WIDTH, bytes_accessed=8 << 20, transcendentals=0
        ),
    )(routes, pick, mixed, returned, residual, att, grad)


def pass_kernel(*refs):
    pass


def after(earlier, *values):
    anywhere = pl.BlockSpec(memory_space=pl.ANY)
    return pl.pallas_call(
        pass_kernel,
        in_specs=[anywhere] * (1 + len(values)),
        out_specs=[anywhere] * len(values),
        out_shape=[jax.ShapeDtypeStruct(v.shape, v.dtype) for v in values],
        input_output_aliases={1 + i: i for i in range(len(values))},
    )(earlier, *values)


def exchange(blocks):
    return lax.all_to_all(
        blocks, ("seq", "expert"), 0, 0, tiled=True, axis_index_groups=PLANE_GROUPS
    )


def exchange_rows(rows):
    return exchange(rows.reshape(EXPERTS, HALF, WIDTH)).reshape(PART, WIDTH)


def swap_cores(values):
    return lax.ppermute(values, "seq", [(i, i ^ 1) for i in range(SEQ)])


def send_earlier(values, planes):
    pairs = [
        (2 * z + core, 2 * (z + planes - PLANES) + core)
        for z in range(PLANES - planes, PLANES)
        for core in range(2)
    ]
    return lax.ppermute(values, "seq", pairs)


def on_device(
    residual,
    queries,
    key_input,
    value_input,
    routes,
    mix_weights,
    gate_weight,
    up_weight,
    down_weight,
    grad_out,
):
    seq = lax.axis_index("seq")
    seq_index = seq.astype(jnp.int32).reshape(1)
    core = (seq & 1).astype(jnp.int32)
    core_index = core.reshape(1)
    residual = residual.reshape(TOK, WIDTH)
    queries = queries.reshape(TOK, WIDTH)
    grad = grad_out.reshape(TOK, WIDTH)
    routes = jnp.transpose(routes, (2, 0, 1))
    mix = jnp.transpose(mix_weights, (2, 0, 1))
    gate_w = jnp.swapaxes(gate_weight, 1, 2)
    up_w = jnp.swapaxes(up_weight, 1, 2)
    pairs = jnp.concatenate(
        [key_input.reshape(TOK, KV_WIDTH), value_input.reshape(TOK, KV_WIDTH)], axis=1
    )
    pairs = lax.all_gather(pairs, "seq", axis=0, tiled=True)
    pick, mixed, grad_rows = make_plan(routes, mix, grad)
    grad_rows = exchange(grad_rows)
    att, lse, rows_a, rows_b = attend(seq_index, queries, pairs, residual, pick)
    rows_a, rows_b = after(grad_rows, rows_a, rows_b)
    rows_a = exchange_rows(rows_a)
    (rows_b,) = after(rows_a, rows_b)
    rows_b = exchange_rows(rows_b)
    weights = (gate_w, up_w, down_weight)
    back_a, act_a, gate_a, up_a = expert_rows(0, core_index, rows_a, grad_rows, *weights)
    back_a = exchange_rows(back_a)
    gate_pre, up_pre, act_b = expert_forward(core_index, rows_b, gate_w, up_w)
    down_keep, down_send = column_sums(down_kernel, 2, core_index, (grad_rows,), (act_a, act_b))
    down_stack = stack_experts(core_index, down_keep, swap_cores(down_send))
    (gate_pre,) = after(down_stack, gate_pre)
    back_b, gate_b, up_b = expert_backward(1, core_index, gate_pre, up_pre, grad_rows, *weights)
    back_b = exchange_rows(back_b)
    gate_a, gate_b = after(down_stack, gate_a, gate_b)
    gate_keep, gate_send, up_keep, up_send = column_sums(
        inner_kernel, 4, core_index, (rows_a, rows_b), (gate_a, gate_b, up_a, up_b)
    )
    results = exchange(expert_results(core_index, (act_a, act_b), down_weight))
    gate_stack = stack_experts(core_index, gate_keep, swap_cores(gate_send))
    up_stack = stack_experts(core_index, up_keep, swap_cores(up_send))
    (lse,) = after(gate_stack, lse)
    (lse,) = after(up_stack, lse)
    res_grad, query_grad, keep, send = attend_back(
        seq_index, queries, pairs, lse, back_a, back_b, pick, residual, att, grad
    )
    other = swap_cores(send)
    parts = [
        (keep[d].astype(f32) + other[d].astype(f32)).astype(bf16) for d in range(PLANES)
    ]
    kv_grad = parts[0].astype(f32)
    for d in range(1, PLANES):
        kv_grad = kv_grad + send_earlier(parts[d], d).astype(f32)
    kv_grad = kv_grad.astype(bf16)
    layer_out, mix_grad = combine(routes, pick, mixed, results, residual, att, grad)
    weight_grads = []
    for stacked in (down_stack, gate_stack, up_stack):
        share = lax.psum_scatter(
            stacked.reshape(PLANES * 2 * HIDDEN, OWN),
            "seq",
            scatter_dimension=0,
            axis_index_groups=Z_GROUPS,
            tiled=True,
        )
        weight_grads.append(share.reshape(2, HIDDEN, OWN))
    down_grad, gate_grad, up_grad = weight_grads
    return (
        layer_out.reshape(1, TOK, WIDTH),
        res_grad.reshape(1, TOK, WIDTH),
        query_grad.reshape(1, TOK, WIDTH),
        kv_grad[:, :KV_WIDTH].reshape(1, TOK, KV_WIDTH),
        kv_grad[:, KV_WIDTH:].reshape(1, TOK, KV_WIDTH),
        jnp.transpose(mix_grad, (1, 2, 0)),
        jnp.swapaxes(gate_grad, 1, 2),
        jnp.swapaxes(up_grad, 1, 2),
        down_grad,
    )


def solution(mesh):
    rows = P("expert", "seq", None)
    weights = P("expert", None, None)
    return jax.shard_map(
        on_device,
        mesh=mesh,
        in_specs=(rows, rows, rows, rows, rows, rows, weights, weights, weights, rows),
        out_specs=(rows, rows, rows, rows, rows, rows, rows, rows, P("expert", None, "seq")),
        check_vma=False,
    )
```

```python
import math

import jax
import jax.numpy as jnp
from jax import lax
from jax.experimental import pallas as pl
from jax.experimental.pallas import tpu as pltpu
from jax.sharding import PartitionSpec as P

DH = 128
TOK = 128
WIDTH = 2048
HEADS = 16
KV_HEADS = 4
GROUP = 4
KV_WIDTH = 512
TOP = 6
SEQ = 8
PLANES = 4
RANKS = 16
EXPERTS = 32
SLOTS = 32
HALF = 16
ROWS = EXPERTS * SLOTS
PART = EXPERTS * HALF
OWN = WIDTH // SEQ
HIDDEN = 704
FULL = TOK * SEQ
SCALE = 1.0 / math.sqrt(DH)
NEG_BIG = -1e30
NORM_EPS = 1e-06
VMEM_BYTES = 56 * 1024 * 1024

bf16 = jnp.bfloat16
f32 = jnp.float32

PLANE_GROUPS = [
    [(2 * z + core) * RANKS + rank for core in range(2) for rank in range(RANKS)]
    for z in range(PLANES)
]
Z_GROUPS = [[2 * z + core for z in range(PLANES)] for core in range(2)]


def params(**kw):
    return pltpu.CompilerParams(vmem_limit_bytes=VMEM_BYTES, **kw)


def cost(share, flops, bytes_accessed, transcendentals):
    return pl.CostEstimate(
        flops=share * flops, bytes_accessed=share * bytes_accessed, transcendentals=transcendentals
    )


def whole(shape):
    return pl.BlockSpec(shape, lambda *_: (0,) * len(shape))


def dot_nn(a, b):
    return lax.dot_general(a, b, (((1,), (0,)), ((), ())), preferred_element_type=f32)


def dot_nt(a, b):
    return lax.dot_general(a, b, (((1,), (1,)), ((), ())), preferred_element_type=f32)


def dot_tn(a, b):
    return lax.dot_general(a, b, (((0,), (0,)), ((), ())), preferred_element_type=f32)


def expert_ids():
    row = lax.broadcasted_iota(jnp.int32, (EXPERTS, TOK), 0)
    return 2 * (row & (RANKS - 1)) + (row >> 4)


def plan_kernel(routes, mix, grad, pick_out, mixed_out, rows_out):
    ids = expert_ids()
    member = jnp.zeros((EXPERTS, TOK), f32)
    weight = jnp.zeros((EXPERTS, TOK), f32)
    for c in range(TOP):
        hit = routes[c] == ids
        member = member + jnp.where(hit, 1.0, 0.0)
        weight = weight + jnp.where(hit, mix[c], 0.0)
    before = lax.broadcasted_iota(jnp.int32, (TOK, TOK), 0) < lax.broadcasted_iota(
        jnp.int32, (TOK, TOK), 1
    )
    rank = dot_nn(member.astype(bf16), jnp.where(before, 1.0, 0.0).astype(bf16))
    slot = jnp.where(member > 0.0, rank, -1.0)
    place = lax.broadcasted_iota(jnp.int32, (EXPERTS, HALF, TOK), 1).astype(f32)
    for h in range(2):
        pick = jnp.where(slot[:, None, :] == place + float(h * HALF), 1.0, 0.0)
        mixed = (pick * weight[:, None, :]).reshape(PART, TOK)
        pick = pick.reshape(PART, TOK).astype(bf16)
        pick_out[h] = pick
        mixed_out[h] = mixed
        scale = jnp.sum(mixed, axis=1, keepdims=True)
        for i in range(0, PART, 256):
            rows = dot_nn(pick[i : i + 256], grad[...])
            rows = (rows * scale[i : i + 256]).astype(bf16)
            first = i // HALF
            rows_out[first : first + 256 // HALF, h] = rows.reshape(256 // HALF, HALF, WIDTH)


def make_plan(routes, mix, grad):
    return pl.pallas_call(
        plan_kernel,
        out_shape=(
            jax.ShapeDtypeStruct((2, PART, TOK), bf16),
            jax.ShapeDtypeStruct((2, PART, TOK), f32),
            jax.ShapeDtypeStruct((EXPERTS, 2, HALF, WIDTH), bf16),
        ),
        compiler_params=params(),
        cost_estimate=cost(1,
            flops=2 * ROWS * TOK * WIDTH, bytes_accessed=8 << 20, transcendentals=0
        ),
    )(routes, mix, grad)


def visible_keys(seq_ref):
    row = seq_ref[0] * TOK + lax.broadcasted_iota(jnp.int32, (TOK, FULL), 0)
    return lax.broadcasted_iota(jnp.int32, (TOK, FULL), 1) <= row


def norm_parts(residual, attention):
    hidden = residual.astype(f32) + attention.astype(f32)
    inv_rms = lax.rsqrt(jnp.mean(hidden * hidden, axis=1, keepdims=True) + NORM_EPS)
    return hidden, inv_rms


def attend_kernel(
    seq_ref, q_ref, k_ref, v_ref, residual, pick, att_out, lse_out, first_out, second_out
):
    head = pl.program_id(0)
    keys, values = k_ref[...], v_ref[...]
    visible = visible_keys(seq_ref)
    outs, totals = [], []
    for g in range(GROUP):
        scores = dot_nt(q_ref[:, g * DH : (g + 1) * DH], keys) * SCALE
        masked = jnp.where(visible, scores, NEG_BIG)
        row_max = jnp.max(masked, axis=1, keepdims=True)
        weights = jnp.exp(masked - row_max)
        row_sum = jnp.sum(weights, axis=1, keepdims=True)
        mixed = dot_nn(weights.astype(bf16), values)
        outs.append((mixed / row_sum).astype(bf16))
        totals.append(jnp.broadcast_to(row_max + jnp.log(row_sum), (TOK, DH)))
    columns = pl.ds(pl.multiple_of(head * GROUP * DH, GROUP * DH), GROUP * DH)
    att_out[:, columns] = jnp.concatenate(outs, axis=1)
    lse_out[...] = jnp.concatenate(totals, axis=1)

    @pl.when(head == KV_HEADS - 1)
    def _():
        hidden, inv_rms = norm_parts(residual[...], att_out[...])
        normed = (hidden * inv_rms).astype(bf16)
        for h, rows_out in enumerate((first_out, second_out)):
            for i in range(0, PART, 256):
                rows_out[i : i + 256, :] = dot_nn(pick[h, i : i + 256, :], normed).astype(bf16)


def attend(seq_index, queries, pairs, residual, pick):
    return pl.pallas_call(
        attend_kernel,
        grid_spec=pltpu.PrefetchScalarGridSpec(
            num_scalar_prefetch=1,
            grid=(KV_HEADS,),
            in_specs=[
                pl.BlockSpec((TOK, GROUP * DH), lambda h, s: (0, h)),
                pl.BlockSpec((FULL, DH), lambda h, s: (0, h)),
                pl.BlockSpec((FULL, DH), lambda h, s: (0, KV_HEADS + h)),
                whole((TOK, WIDTH)),
                whole((2, PART, TOK)),
            ],
            out_specs=[
                whole((TOK, WIDTH)),
                pl.BlockSpec((TOK, GROUP * DH), lambda h, s: (0, h)),
                whole((PART, WIDTH)),
                whole((PART, WIDTH)),
            ],
        ),
        out_shape=(
            jax.ShapeDtypeStruct((TOK, WIDTH), bf16),
            jax.ShapeDtypeStruct((TOK, WIDTH), f32),
            jax.ShapeDtypeStruct((PART, WIDTH), bf16),
            jax.ShapeDtypeStruct((PART, WIDTH), bf16),
        ),
        compiler_params=params(),
        cost_estimate=cost(1,
            flops=4 * TOK * FULL * WIDTH + 2 * ROWS * TOK * WIDTH,
            bytes_accessed=10 << 20,
            transcendentals=HEADS * TOK * FULL,
        ),
    )(seq_index, queries, pairs, pairs, residual, pick)


def expert_kernel(core, rows, pairs, gate_w, up_w, down_w, back_out, act_out, gate_out, up_out):
    step = rows.shape[0]
    gate = dot_nt(rows[...], gate_w[0])
    up = dot_nt(rows[...], up_w[0])
    sig = jax.nn.sigmoid(gate)
    silu = gate * sig
    act_out[...] = (silu * up).astype(bf16)
    act_grad = dot_nt(pairs[...].reshape(step, WIDTH), down_w[0])
    gate_grad = (act_grad * up * sig * (1.0 + gate * (1.0 - sig))).astype(bf16)
    up_grad = (act_grad * silu).astype(bf16)
    gate_out[...] = gate_grad
    up_out[...] = up_grad
    back_out[...] = (dot_nn(gate_grad, gate_w[0]) + dot_nn(up_grad, up_w[0])).astype(bf16)


def expert_rows(half, core, rows, pairs, gate_w, up_w, down_w):
    step = 256
    tile = pl.BlockSpec((step, WIDTH), lambda i, c: (i, 0))
    thin = pl.BlockSpec((step, HIDDEN), lambda i, c: (i, 0))
    weight = pl.BlockSpec(
        (1, HIDDEN, WIDTH), lambda i, c: (c[0], 0, 0), pipeline_mode=pl.Buffered(1)
    )
    return pl.pallas_call(
        expert_kernel,
        grid_spec=pltpu.PrefetchScalarGridSpec(
            num_scalar_prefetch=1,
            grid=(PART // step,),
            in_specs=[
                tile,
                pl.BlockSpec((step // HALF, 1, HALF, WIDTH), lambda i, c: (i, half, 0, 0)),
                weight,
                weight,
                weight,
            ],
            out_specs=[tile, thin, thin, thin],
        ),
        out_shape=(
            jax.ShapeDtypeStruct((PART, WIDTH), bf16),
            jax.ShapeDtypeStruct((PART, HIDDEN), bf16),
            jax.ShapeDtypeStruct((PART, HIDDEN), bf16),
            jax.ShapeDtypeStruct((PART, HIDDEN), bf16),
        ),
        compiler_params=params(),
        cost_estimate=cost(100,
            flops=10 * PART * HIDDEN * WIDTH,
            bytes_accessed=16 << 20,
            transcendentals=PART * HIDDEN,
        ),
    )(core, rows, pairs, gate_w, up_w, down_w)


def forward_kernel(core, rows, gate_w, up_w, gate_out, up_out, act_out):
    gate = dot_nt(rows[...], gate_w[0])
    up = dot_nt(rows[...], up_w[0])
    gate_out[...] = gate
    up_out[...] = up
    act_out[...] = (gate * jax.nn.sigmoid(gate) * up).astype(bf16)


def backward_kernel(core, gate_in, up_in, pairs, gate_w, up_w, down_w, back_out, gate_out, up_out):
    step = gate_in.shape[0]
    gate, up = gate_in[...], up_in[...]
    sig = jax.nn.sigmoid(gate)
    act_grad = dot_nt(pairs[...].reshape(step, WIDTH), down_w[0])
    gate_grad = (act_grad * up * sig * (1.0 + gate * (1.0 - sig))).astype(bf16)
    up_grad = (act_grad * gate * sig).astype(bf16)
    gate_out[...] = gate_grad
    up_out[...] = up_grad
    back_out[...] = (dot_nn(gate_grad, gate_w[0]) + dot_nn(up_grad, up_w[0])).astype(bf16)


def expert_forward(core, rows, gate_w, up_w):
    step = 256
    thin = pl.BlockSpec((step, HIDDEN), lambda i, c: (i, 0))
    weight = pl.BlockSpec(
        (1, HIDDEN, WIDTH), lambda i, c: (c[0], 0, 0), pipeline_mode=pl.Buffered(1)
    )
    return pl.pallas_call(
        forward_kernel,
        grid_spec=pltpu.PrefetchScalarGridSpec(
            num_scalar_prefetch=1,
            grid=(PART // step,),
            in_specs=[pl.BlockSpec((step, WIDTH), lambda i, c: (i, 0)), weight, weight],
            out_specs=[thin, thin, thin],
        ),
        out_shape=(
            jax.ShapeDtypeStruct((PART, HIDDEN), f32),
            jax.ShapeDtypeStruct((PART, HIDDEN), f32),
            jax.ShapeDtypeStruct((PART, HIDDEN), bf16),
        ),
        compiler_params=params(),
        cost_estimate=cost(100,
            flops=4 * PART * HIDDEN * WIDTH,
            bytes_accessed=10 << 20,
            transcendentals=PART * HIDDEN,
        ),
    )(core, rows, gate_w, up_w)


def expert_backward(half, core, gate, up, pairs, gate_w, up_w, down_w):
    step = 256
    tile = pl.BlockSpec((step, WIDTH), lambda i, c: (i, 0))
    thin = pl.BlockSpec((step, HIDDEN), lambda i, c: (i, 0))
    weight = pl.BlockSpec(
        (1, HIDDEN, WIDTH), lambda i, c: (c[0], 0, 0), pipeline_mode=pl.Buffered(1)
    )
    return pl.pallas_call(
        backward_kernel,
        grid_spec=pltpu.PrefetchScalarGridSpec(
            num_scalar_prefetch=1,
            grid=(PART // step,),
            in_specs=[
                thin,
                thin,
                pl.BlockSpec((step // HALF, 1, HALF, WIDTH), lambda i, c: (i, half, 0, 0)),
                weight,
                weight,
                weight,
            ],
            out_specs=[tile, thin, thin],
        ),
        out_shape=(
            jax.ShapeDtypeStruct((PART, WIDTH), bf16),
            jax.ShapeDtypeStruct((PART, HIDDEN), bf16),
            jax.ShapeDtypeStruct((PART, HIDDEN), bf16),
        ),
        compiler_params=params(),
        cost_estimate=cost(100,
            flops=6 * PART * HIDDEN * WIDTH,
            bytes_accessed=16 << 20,
            transcendentals=PART * HIDDEN,
        ),
    )(core, gate, up, pairs, gate_w, up_w, down_w)


def split_columns(place, total, value, keep_out, send_out):
    total[...] = value
    keep = pl.ds(pl.multiple_of(place * OWN, OWN), OWN)
    send = pl.ds(pl.multiple_of((1 - place) * OWN, OWN), OWN)
    keep_out[0] = total[:, keep].astype(bf16)
    send_out[0] = total[:, send].astype(bf16)


def down_kernel(core, pairs, act_a, act_b, keep, send, total):
    pairs_a = pairs[:, 0].reshape(PART, 2 * OWN)
    pairs_b = pairs[:, 1].reshape(PART, 2 * OWN)
    value = dot_tn(act_a[...], pairs_a) + dot_tn(act_b[...], pairs_b)
    split_columns(core[0], total, value, keep, send)


def inner_kernel(
    core, rows_a, rows_b, gate_a, gate_b, up_a, up_b, gate_keep, gate_send, up_keep, up_send, total
):
    value = dot_tn(gate_a[...], rows_a[...]) + dot_tn(gate_b[...], rows_b[...])
    split_columns(core[0], total, value, gate_keep, gate_send)
    value = dot_tn(up_a[...], rows_a[...]) + dot_tn(up_b[...], rows_b[...])
    split_columns(core[0], total, value, up_keep, up_send)


def column_sums(kernel, n_outs, core, wide, thin):
    columns = [
        pl.BlockSpec((PART, 2 * OWN), lambda i, c: (0, i))
        if w.ndim == 2
        else pl.BlockSpec((EXPERTS, 2, HALF, 2 * OWN), lambda i, c: (0, 0, 0, i))
        for w in wide
    ]
    out = pl.BlockSpec((1, HIDDEN, OWN), lambda i, c: (i, 0, 0))
    return pl.pallas_call(
        kernel,
        grid_spec=pltpu.PrefetchScalarGridSpec(
            num_scalar_prefetch=1,
            grid=(PLANES,),
            in_specs=columns + [whole((PART, HIDDEN))] * len(thin),
            out_specs=[out] * n_outs,
            scratch_shapes=[pltpu.VMEM((HIDDEN, 2 * OWN), f32)],
        ),
        out_shape=(jax.ShapeDtypeStruct((PLANES, HIDDEN, OWN), bf16),) * n_outs,
        compiler_params=params(),
        cost_estimate=cost(100,
            flops=n_outs * ROWS * HIDDEN * WIDTH,
            bytes_accessed=n_outs * (4 << 20),
            transcendentals=0,
        ),
    )(core, *wide, *thin)


def stack_kernel(core, keep, other, out):
    out[0, core[0]] = keep[0]
    out[0, 1 - core[0]] = other[0]


def stack_experts(core, keep, other):
    block = pl.BlockSpec((1, HIDDEN, OWN), lambda i, c: (i, 0, 0))
    return pl.pallas_call(
        stack_kernel,
        grid_spec=pltpu.PrefetchScalarGridSpec(
            num_scalar_prefetch=1,
            grid=(PLANES,),
            in_specs=[block, block],
            out_specs=pl.BlockSpec((1, 2, HIDDEN, OWN), lambda i, c: (i, 0, 0, 0)),
        ),
        out_shape=jax.ShapeDtypeStruct((PLANES, 2, HIDDEN, OWN), bf16),
        compiler_params=params(),
        cost_estimate=cost(100, flops=0, bytes_accessed=6 << 20, transcendentals=0),
    )(core, keep, other)


def result_kernel(core, act_a, act_b, down_w, out):
    rows = act_a.shape[0]
    out[:, 0] = dot_nn(act_a[...], down_w[0]).astype(bf16).reshape(rows // HALF, HALF, WIDTH)
    out[:, 1] = dot_nn(act_b[...], down_w[0]).astype(bf16).reshape(rows // HALF, HALF, WIDTH)


def expert_results(core, act, down_w):
    step = 128
    return pl.pallas_call(
        result_kernel,
        grid_spec=pltpu.PrefetchScalarGridSpec(
            num_scalar_prefetch=1,
            grid=(PART // step,),
            in_specs=[
                pl.BlockSpec((step, HIDDEN), lambda i, c: (i, 0)),
                pl.BlockSpec((step, HIDDEN), lambda i, c: (i, 0)),
                pl.BlockSpec((1, HIDDEN, WIDTH), lambda i, c: (c[0], 0, 0)),
            ],
            out_specs=pl.BlockSpec((step // HALF, 2, HALF, WIDTH), lambda i, c: (i, 0, 0, 0)),
        ),
        out_shape=jax.ShapeDtypeStruct((EXPERTS, 2, HALF, WIDTH), bf16),
        compiler_params=params(),
        cost_estimate=cost(100,
            flops=2 * ROWS * HIDDEN * WIDTH, bytes_accessed=9 << 20, transcendentals=0
        ),
    )(core, *act, down_w)


def attend_back_kernel(
    seq_ref,
    q_ref,
    k_ref,
    v_ref,
    lse,
    back_a,
    back_b,
    pick,
    residual,
    att,
    grad,
    res_out,
    q_out,
    keep_out,
    send_out,
    kv_sum,
):
    head = pl.program_id(0)

    @pl.when(head == 0)
    def _():
        normed_grad = dot_tn(pick[0], back_a[...]) + dot_tn(pick[1], back_b[...])
        hidden, inv_rms = norm_parts(residual[...], att[...])
        normed = hidden * inv_rms
        dot_mean = jnp.mean(normed_grad * normed, axis=1, keepdims=True)
        total = grad[...].astype(f32) + inv_rms * (normed_grad - normed * dot_mean)
        res_out[...] = total.astype(bf16)

    keys, values = k_ref[...], v_ref[...]
    visible = visible_keys(seq_ref)
    score_parts, prob_parts, query_parts, grad_parts = [], [], [], []
    for g in range(GROUP):
        query = q_ref[:, g * DH : (g + 1) * DH]
        columns = pl.ds(pl.multiple_of(head * GROUP * DH + g * DH, DH), DH)
        out_grad = res_out[:, columns]
        delta = jnp.sum(
            out_grad.astype(f32) * att[:, columns].astype(f32), axis=1, keepdims=True
        )
        scores = dot_nt(query, keys) * SCALE
        total = lse[:, g * DH : g * DH + 1]
        probs = jnp.exp(jnp.where(visible, scores - total, NEG_BIG))
        prob_grad = dot_nt(out_grad, values)
        score_grad = (probs * (prob_grad - delta)).astype(bf16)
        q_out[:, g * DH : (g + 1) * DH] = (dot_nn(score_grad, keys) * SCALE).astype(bf16)
        score_parts.append(score_grad)
        prob_parts.append(probs.astype(bf16))
        query_parts.append(query)
        grad_parts.append(out_grad)
    key_sum = dot_tn(jnp.concatenate(score_parts, axis=0), jnp.concatenate(query_parts, axis=0))
    value_sum = dot_tn(jnp.concatenate(prob_parts, axis=0), jnp.concatenate(grad_parts, axis=0))
    kv_sum[:, pl.ds(pl.multiple_of(head * DH, DH), DH)] = (key_sum * SCALE).astype(bf16)
    kv_sum[:, pl.ds(pl.multiple_of(KV_WIDTH + head * DH, DH), DH)] = value_sum.astype(bf16)

    @pl.when(head == KV_HEADS - 1)
    def _():
        plane, core = seq_ref[0] >> 1, seq_ref[0] & 1
        for d in range(PLANES):
            mine = 2 * ((plane + d) & (PLANES - 1)) + core
            keep_out[d] = kv_sum[pl.ds(pl.multiple_of(mine * TOK, TOK), TOK), :]
            send_out[d] = kv_sum[pl.ds(pl.multiple_of((mine ^ 1) * TOK, TOK), TOK), :]


def attend_back(seq_index, queries, pairs, lse, back_a, back_b, pick, residual, att, grad):
    return pl.pallas_call(
        attend_back_kernel,
        grid_spec=pltpu.PrefetchScalarGridSpec(
            num_scalar_prefetch=1,
            grid=(KV_HEADS,),
            in_specs=[
                pl.BlockSpec((TOK, GROUP * DH), lambda h, s: (0, h)),
                pl.BlockSpec((FULL, DH), lambda h, s: (0, h)),
                pl.BlockSpec((FULL, DH), lambda h, s: (0, KV_HEADS + h)),
                pl.BlockSpec((TOK, GROUP * DH), lambda h, s: (0, h)),
                whole((PART, WIDTH)),
                whole((PART, WIDTH)),
                whole((2, PART, TOK)),
                whole((TOK, WIDTH)),
                whole((TOK, WIDTH)),
                whole((TOK, WIDTH)),
            ],
            out_specs=[
                whole((TOK, WIDTH)),
                pl.BlockSpec((TOK, GROUP * DH), lambda h, s: (0, h)),
                whole((PLANES, TOK, 2 * KV_WIDTH)),
                whole((PLANES, TOK, 2 * KV_WIDTH)),
            ],
            scratch_shapes=[pltpu.VMEM((FULL, 2 * KV_WIDTH), bf16)],
        ),
        out_shape=(
            jax.ShapeDtypeStruct((TOK, WIDTH), bf16),
            jax.ShapeDtypeStruct((TOK, WIDTH), bf16),
            jax.ShapeDtypeStruct((PLANES, TOK, 2 * KV_WIDTH), bf16),
            jax.ShapeDtypeStruct((PLANES, TOK, 2 * KV_WIDTH), bf16),
        ),
        compiler_params=params(),
        cost_estimate=cost(100,
            flops=10 * TOK * FULL * WIDTH + 2 * ROWS * TOK * WIDTH,
            bytes_accessed=12 << 20,
            transcendentals=HEADS * TOK * FULL,
        ),
    )(seq_index, queries, pairs, pairs, lse, back_a, back_b, pick, residual, att, grad)


def combine_kernel(
    routes, pick, mixed, returned, residual, att, grad, layer_out, mix_out, by_expert
):
    step = pl.program_id(0)

    @pl.when(step == 0)
    def _():
        by_expert[...] = jnp.zeros_like(by_expert)

    total = residual[...].astype(f32) + att[...].astype(f32)
    for h in range(2):
        rows = returned[:, h].reshape(PART, -1)
        coarse = mixed[h].astype(bf16)
        fine = (mixed[h] - coarse.astype(f32)).astype(bf16)
        total = total + dot_tn(coarse, rows) + dot_tn(fine, rows)
        inner = dot_nt(rows, grad[...]) * pick[h].astype(f32)
        by_expert[...] += jnp.sum(inner.reshape(EXPERTS, HALF, TOK), axis=1)
    layer_out[...] = total.astype(bf16)

    @pl.when(step == pl.num_programs(0) - 1)
    def _():
        ids = expert_ids()
        for c in range(TOP):
            hit = routes[c] == ids
            mix_out[c] = jnp.sum(jnp.where(hit, by_expert[...], 0.0), axis=0, keepdims=True)


def combine(routes, pick, mixed, returned, residual, att, grad):
    part = WIDTH // 4
    columns = pl.BlockSpec((TOK, part), lambda i: (0, i))
    return pl.pallas_call(
        combine_kernel,
        grid=(4,),
        in_specs=[
            whole((TOP, 1, TOK)),
            whole((2, PART, TOK)),
            whole((2, PART, TOK)),
            pl.BlockSpec((EXPERTS, 2, HALF, part), lambda i: (0, 0, 0, i)),
            columns,
            columns,
            columns,
        ],
        out_specs=[columns, whole((TOP, 1, TOK))],
        out_shape=(
            jax.ShapeDtypeStruct((TOK, WIDTH), bf16),
            jax.ShapeDtypeStruct((TOP, 1, TOK), f32),
        ),
        scratch_shapes=[pltpu.VMEM((EXPERTS, TOK), f32)],
        compiler_params=params(),
        cost_estimate=cost(100, flops=6 * ROWS * TOK * WIDTH, bytes_accessed=8 << 20, transcendentals=0
        ),
    )(routes, pick, mixed, returned, residual, att, grad)


def pass_kernel(*refs):
    pass


def after(earlier, *values):
    anywhere = pl.BlockSpec(memory_space=pl.ANY)
    return pl.pallas_call(
        pass_kernel,
        in_specs=[anywhere] * (1 + len(values)),
        out_specs=[anywhere] * len(values),
        out_shape=[jax.ShapeDtypeStruct(v.shape, v.dtype) for v in values],
        input_output_aliases={1 + i: i for i in range(len(values))},
    )(earlier, *values)


def exchange(blocks):
    return lax.all_to_all(
        blocks, ("seq", "expert"), 0, 0, tiled=True, axis_index_groups=PLANE_GROUPS
    )


def exchange_rows(rows):
    return exchange(rows.reshape(EXPERTS, HALF, WIDTH)).reshape(PART, WIDTH)


def swap_cores(values):
    return lax.ppermute(values, "seq", [(i, i ^ 1) for i in range(SEQ)])


def send_earlier(values, planes):
    pairs = [
        (2 * z + core, 2 * (z + planes - PLANES) + core)
        for z in range(PLANES - planes, PLANES)
        for core in range(2)
    ]
    return lax.ppermute(values, "seq", pairs)


def on_device(
    residual,
    queries,
    key_input,
    value_input,
    routes,
    mix_weights,
    gate_weight,
    up_weight,
    down_weight,
    grad_out,
):
    seq = lax.axis_index("seq")
    seq_index = seq.astype(jnp.int32).reshape(1)
    core = (seq & 1).astype(jnp.int32)
    core_index = core.reshape(1)
    residual = residual.reshape(TOK, WIDTH)
    queries = queries.reshape(TOK, WIDTH)
    grad = grad_out.reshape(TOK, WIDTH)
    routes = jnp.transpose(routes, (2, 0, 1))
    mix = jnp.transpose(mix_weights, (2, 0, 1))
    gate_w = jnp.swapaxes(gate_weight, 1, 2)
    up_w = jnp.swapaxes(up_weight, 1, 2)
    pairs = jnp.concatenate(
        [key_input.reshape(TOK, KV_WIDTH), value_input.reshape(TOK, KV_WIDTH)], axis=1
    )
    pairs = lax.all_gather(pairs, "seq", axis=0, tiled=True)
    pick, mixed, grad_rows = make_plan(routes, mix, grad)
    grad_rows = exchange(grad_rows)
    att, lse, rows_a, rows_b = attend(seq_index, queries, pairs, residual, pick)
    rows_a, rows_b = after(grad_rows, rows_a, rows_b)
    rows_a = exchange_rows(rows_a)
    (rows_b,) = after(rows_a, rows_b)
    rows_b = exchange_rows(rows_b)
    weights = (gate_w, up_w, down_weight)
    back_a, act_a, gate_a, up_a = expert_rows(0, core_index, rows_a, grad_rows, *weights)
    back_a = exchange_rows(back_a)
    gate_pre, up_pre, act_b = expert_forward(core_index, rows_b, gate_w, up_w)
    down_keep, down_send = column_sums(down_kernel, 2, core_index, (grad_rows,), (act_a, act_b))
    down_stack = stack_experts(core_index, down_keep, swap_cores(down_send))
    (gate_pre,) = after(down_stack, gate_pre)
    back_b, gate_b, up_b = expert_backward(1, core_index, gate_pre, up_pre, grad_rows, *weights)
    back_b = exchange_rows(back_b)
    gate_a, gate_b = after(down_stack, gate_a, gate_b)
    gate_keep, gate_send, up_keep, up_send = column_sums(
        inner_kernel, 4, core_index, (rows_a, rows_b), (gate_a, gate_b, up_a, up_b)
    )
    results = exchange(expert_results(core_index, (act_a, act_b), down_weight))
    gate_stack = stack_experts(core_index, gate_keep, swap_cores(gate_send))
    up_stack = stack_experts(core_index, up_keep, swap_cores(up_send))
    (lse,) = after(gate_stack, lse)
    (lse,) = after(up_stack, lse)
    res_grad, query_grad, keep, send = attend_back(
        seq_index, queries, pairs, lse, back_a, back_b, pick, residual, att, grad
    )
    other = swap_cores(send)
    parts = [
        (keep[d].astype(f32) + other[d].astype(f32)).astype(bf16) for d in range(PLANES)
    ]
    kv_grad = parts[0].astype(f32)
    for d in range(1, PLANES):
        kv_grad = kv_grad + send_earlier(parts[d], d).astype(f32)
    kv_grad = kv_grad.astype(bf16)
    layer_out, mix_grad = combine(routes, pick, mixed, results, residual, att, grad)
    weight_grads = []
    for stacked in (down_stack, gate_stack, up_stack):
        share = lax.psum_scatter(
            stacked.reshape(PLANES * 2 * HIDDEN, OWN),
            "seq",
            scatter_dimension=0,
            axis_index_groups=Z_GROUPS,
            tiled=True,
        )
        weight_grads.append(share.reshape(2, HIDDEN, OWN))
    down_grad, gate_grad, up_grad = weight_grads
    return (
        layer_out.reshape(1, TOK, WIDTH),
        res_grad.reshape(1, TOK, WIDTH),
        query_grad.reshape(1, TOK, WIDTH),
        kv_grad[:, :KV_WIDTH].reshape(1, TOK, KV_WIDTH),
        kv_grad[:, KV_WIDTH:].reshape(1, TOK, KV_WIDTH),
        jnp.transpose(mix_grad, (1, 2, 0)),
        jnp.swapaxes(gate_grad, 1, 2),
        jnp.swapaxes(up_grad, 1, 2),
        down_grad,
    )


def solution(mesh):
    rows = P("expert", "seq", None)
    weights = P("expert", None, None)
    return jax.shard_map(
        on_device,
        mesh=mesh,
        in_specs=(rows, rows, rows, rows, rows, rows, weights, weights, weights, rows),
        out_specs=(rows, rows, rows, rows, rows, rows, rows, rows, P("expert", None, "seq")),
        check_vma=False,
    )
```
